128 devices in a mesh: comp: 2 (over z_lo), ty: 8 (over y, z_hi), tx: 8 (over x, core).
Axes of the slice: x: 4, y: 4, z: 4 (z_hi: 2, z_lo: 2; z = z_hi * 2 + z_lo), core: 2. Of those that a mesh axis runs over, the one named last changes fastest.
Arguments:
- state: float32 [2, 150, 512, 1024], P('comp', None, 'ty', 'tx'), may hold values from -6 to 6
- diffusivity: float32 [2, 150], P('comp'), may hold values from 0.02 to 0.2
- mixing: float32 [2, 150, 150], P('comp'), may hold values from -0.5 to 0.5
- ocean_mask: int32 [512, 1024], P('ty', 'tx'), may hold values 0 or 1
- flux_dest: int32 [8, 512, 1], P('tx', 'ty'), may hold values from 0 to 63; in each aligned block of 64 rows (0 to 63, 64 to 127, ..., all dimensions but the last counted through in order) at most 2 rows name the same one
- flux_target: int32 [8, 512], P('tx', 'ty'), may hold values from 0 to 63
- flux_weight: float32 [8, 512], P('tx', 'ty'), may hold values from 0.5 to 1.5
- fold_source: int32 [1024], P('tx'), may hold values from 0 to 1023, each once
Outputs:
- final_state: float32 [2, 150, 512, 1024], P('comp', None, 'ty', 'tx')
The draws below stay inside these ranges and needn't reach their ends.
Inputs may be any that keep to these rules, and one draw needn't show every extreme that they name: `flux_dest`: among the 64 rows of one device (aligned blocks of 64 rows in the flattened order) no ocean tile is named more than 2 times. `fold_source`: A permutation of the 1024 columns.
All inputs are finite; a program needn't handle non-finite values. No bound on the sum of `ocean_mask` on one device may be relied on, other than what follows from the above.
Results may differ from the reference program's by a relative error of at most 0.0001.
Values sent between devices are 32-bit elements; how exact they have to be, the bound alone decides.
No kernel may reach another device: no remote copies, remote signals or barrier semaphores. Data moves between devices by JAX's collectives and lax.ppermute only.
A program may use at most 192 MiB of HBM per device.

```python
import math
import jax
import jax.numpy as jnp
import numpy as np
from jax import lax

CY = 64
CX = 128
LEV = 75
C = 150
CAP = 2
NSTEP = 4
INTERVALS = 2
MESH_NORTHWARD_N = 512
MESH_EASTWARD_N = 1024
N_TY = 8
N_TX = 8


def touch_ends(result, rng, smallest, top_value):
    index_at = [jax.random.randint(jax.random.fold_in(rng, axis), (), 0, length) for axis, length in enumerate(result.shape)]
    longest = result.shape.index(max(result.shape))
    beside = index_at[:longest] + [(index_at[longest] + 1) % result.shape[longest]] + index_at[longest + 1:]
    return result.at[tuple(index_at)].set(smallest).at[tuple(beside)].set(top_value)


def level_of(stream_key, shape, shards, smallest, high):
    def one(position, blocks):
        draws = jax.random.uniform(jax.random.fold_in(jax.random.fold_in(stream_key, 6), position), (blocks,), jnp.float32, smallest / len(shards), high / len(shards))
        return jnp.repeat(jnp.exp(draws), shape[position] // blocks).reshape((-1,) + (1,) * (len(shape) - position - 1))

    level = one(*shards[0])
    for cut in shards[1:]:
        level = level * one(*cut)
    return level


def shared_out(own_key, own, number, rows, amount, top, most, skew):
    ranking = jax.random.permutation(own_key, amount)
    heavy_load, usual = shares(amount, rows * top, most, skew, True), shares(amount, rows * top, most, skew, False)
    places = jnp.arange(amount)

    def named(sizes, offset_by):
        used = int((sizes > 0).sum())
        fixed = max(1, used // 4)
        passed = fixed + (places - fixed + offset_by * (used - fixed)) % max(1, amount - fixed)
        return jnp.zeros((amount,), jnp.int32).at[ranking[jnp.where(places < fixed, places, passed)]].set(jnp.asarray(sizes, jnp.int32))

    sizes = jnp.where(number % 4 == 0, named(heavy_load, number // 4), named(usual, number - number // 4 - 1))
    mixed = jax.random.permutation(jax.random.fold_in(own, 3), amount)
    source_of, receiver = mixed[0:amount // 2 * 2:2], mixed[1:amount // 2 * 2:2]
    slack = jnp.minimum(sizes[source_of] - 1, most - sizes[receiver]) // 2
    slack = jnp.where((source_of == ranking[0]) | (receiver == ranking[0]) | (sizes[receiver] == 0), 0, jnp.maximum(slack, 0))
    passed = jax.random.randint(jax.random.fold_in(own, 4), (amount // 2,), 0, 1 << 20) % (slack + 1)
    sizes = sizes.at[source_of].add(-passed).at[receiver].add(passed)
    items = jnp.searchsorted(jnp.cumsum(sizes), jnp.arange(rows * top), side="right").astype(jnp.int32)
    grid = items.reshape(top, rows).T
    grid = grid[jax.random.permutation(jax.random.fold_in(own, 1), rows)]
    offset_by = jax.random.randint(jax.random.fold_in(own, 2), (rows, 1), 0, top)
    return jnp.take_along_axis(grid, (jnp.arange(top)[None, :] + offset_by) % top, axis=1)


def shares(number_of, total, reach, lean, full):
    weights = [(1 << 20) // math.isqrt(grade ** lean) + 1 for grade in range(1, number_of + 1)]
    largest = reach if full else min(reach, max(-(-total // number_of), total * weights[0] // sum(weights)))
    least = 1 if total - largest >= number_of - 1 else 0
    counts, rest = [largest] + [least] * (number_of - 1), total - largest - least * (number_of - 1)
    while rest > 0:
        free = [i for i in range(1, number_of) if counts[i] < largest] or [i for i in range(1, number_of) if counts[i] < reach]
        mass, budget = sum([weights[i] for i in free]), rest
        for i in free:
            more = min(reach - counts[i], max(1, budget * weights[i] // mass), rest)
            counts[i] = counts[i] + more
            rest = rest - more
    return np.array(counts)


def normal_values(stream_key, shape, spread, bound, pieces=(), dtype=jnp.bfloat16):
    values = spread * jax.random.normal(stream_key, shape, jnp.float32)
    if pieces:
        values = values * level_of(stream_key, shape, pieces, -0.22, 0.18)
    return jnp.clip(values, -bound, bound).astype(dtype)


def setup_inputs(seed: int = 0) -> dict:
    keys = jax.random.split(jax.random.key(seed), 9)
    state = normal_values(keys[0], (2, C, MESH_NORTHWARD_N, MESH_EASTWARD_N), 1.0, 6.0, ((0, 2), (2, 8), (3, 8)), jnp.float32)
    diffusivity = jnp.clip(jnp.exp(math.log(0.2) - 2.3025851 * jax.random.uniform(keys[1], (2, C), jnp.float32) ** level_of(keys[1], (2, C), ((0, 2),), -0.2, 0.2)), 0.02, 0.2)
    mixing = normal_values(keys[2], (2, C, C), C ** -0.5, 0.5, ((0, 2),), jnp.float32)
    ocean_mask = touch_ends((jax.random.randint(keys[3], (MESH_NORTHWARD_N, MESH_EASTWARD_N), 0, 4) < 3).astype(jnp.int32), jax.random.fold_in(keys[3], 1), 0, 1)
    flux_dest_keys = jax.random.split(jax.random.fold_in(keys[4], 1), N_TX * MESH_NORTHWARD_N // CY)
    flux_dest_turns = jax.random.permutation(jax.random.fold_in(keys[4], 3), N_TX * MESH_NORTHWARD_N // CY)
    flux_dest = jax.vmap(lambda own, number: shared_out(jax.random.fold_in(keys[4], 2), own, number, CY, N_TY * N_TX, 1, CAP, 2))(flux_dest_keys, flux_dest_turns).reshape((N_TX, MESH_NORTHWARD_N, 1))
    flux_target = touch_ends(jax.random.randint(keys[5], (N_TX, MESH_NORTHWARD_N), 0, CY), jax.random.fold_in(keys[5], 1), 0, CY - 1).astype(jnp.int32)
    flux_weight = jnp.clip(0.5 + 1.0 * jax.random.uniform(keys[6], (N_TX, MESH_NORTHWARD_N), jnp.float32) ** level_of(keys[6], (N_TX, MESH_NORTHWARD_N), ((0, 8), (1, 8)), -0.2, 0.2), 0.5, 1.5)
    fold_source = jax.random.permutation(keys[7], MESH_EASTWARD_N).astype(jnp.int32)
    return {"state": state, "diffusivity": diffusivity, "mixing": mixing, "ocean_mask": ocean_mask, "flux_dest": flux_dest, "flux_target": flux_target, "flux_weight": flux_weight, "fold_source": fold_source}


relaxation_speed = 0.3
flux_gain = 0.25
mix_gain = 0.1


def laplace(current_ocean_snapshot, north_edge):
    east_cells = jnp.roll(current_ocean_snapshot, -1, axis=2)
    west_cells = jnp.roll(current_ocean_snapshot, 1, axis=2)
    north_cells = jnp.concatenate([current_ocean_snapshot[:, 1:], north_edge[:, None]], axis=1)
    south_cells = jnp.concatenate([jnp.zeros_like(current_ocean_snapshot[:, :1]), current_ocean_snapshot[:, :-1]], axis=1)
    return east_cells + west_cells + north_cells + south_cells - 4.0 * current_ocean_snapshot


def pull_uppermost_layer(current_ocean_snapshot):
    return jnp.stack([current_ocean_snapshot[0], current_ocean_snapshot[LEV]])


def advance(current_ocean_snapshot, diffuse, blend_mat, north_edge, forcing, sea_mask):
    tendency = diffuse[:, None, None] * laplace(current_ocean_snapshot, north_edge)
    tendency = tendency + mix_gain * jnp.einsum("ab,byx->ayx", blend_mat, current_ocean_snapshot, precision=lax.Precision.HIGHEST)
    tendency = tendency.at[0].add(forcing[0]).at[LEV].add(forcing[1])
    return current_ocean_snapshot + tendency * sea_mask


def reference(state, diffusivity, mixing, ocean_mask, flux_dest, flux_target, flux_weight, fold_source):
    overlying_air_step = state[0]
    ocean_now = state[1]
    sea_mask = ocean_mask.astype(jnp.float32)
    dest_tile = flux_dest[:, :, 0]
    global_slot = (((dest_tile // N_TX) * CY + flux_target) * N_TX + dest_tile % N_TX).astype(jnp.int32)
    flat_slot = global_slot.reshape(-1)
    for interval in range(INTERVALS):
        air_surface = pull_uppermost_layer(overlying_air_step)
        blocks = air_surface.reshape(2, MESH_NORTHWARD_N, N_TX, CX).transpose(2, 1, 0, 3) * flux_weight[:, :, None, None]
        summed = jax.ops.segment_sum(blocks.reshape(-1, 2, CX), flat_slot, num_segments=MESH_NORTHWARD_N * N_TX)
        flux = summed.reshape(MESH_NORTHWARD_N, N_TX, 2, CX).transpose(2, 0, 1, 3).reshape(2, MESH_NORTHWARD_N, MESH_EASTWARD_N)
        ocean_rows = pull_uppermost_layer(ocean_now).reshape(2, MESH_NORTHWARD_N, N_TX, CX).transpose(1, 2, 0, 3).reshape(MESH_NORTHWARD_N * N_TX, 2, CX)
        collected_entries = jnp.take(ocean_rows, flat_slot, axis=0).reshape(N_TX, MESH_NORTHWARD_N, 2, CX)
        sea_skin_heat = collected_entries.transpose(2, 1, 0, 3).reshape(2, MESH_NORTHWARD_N, MESH_EASTWARD_N)
        for substep in range(NSTEP):
            overlying_air_drive = relaxation_speed * (sea_skin_heat - pull_uppermost_layer(overlying_air_step))
            overlying_air_step = advance(overlying_air_step, diffusivity[0], mixing[0], jnp.zeros_like(overlying_air_step[:, 0]), overlying_air_drive, 1.0)
            fold_edge = jnp.take(ocean_now[:, MESH_NORTHWARD_N - 1, :], fold_source, axis=1)
            ocean_now = advance(ocean_now, diffusivity[1], mixing[1], fold_edge, flux_gain * flux, sea_mask)
    return jnp.stack([overlying_air_step, ocean_now])
```

```python
import functools

import jax
import jax.numpy as jnp
from jax import lax
from jax.experimental import pallas as pl
from jax.experimental.pallas import tpu as pltpu
from jax.sharding import PartitionSpec as P

NSTEP = 4
INTERVALS = 2
H = NSTEP
LANES = 128
CH = 150
CM = 152
CP = 160
MASK, FOLD, FORCE = 152, 153, 154

relaxation_speed = 0.3
flux_gain = 0.25
mix_gain = 0.1

PARAMS = pltpu.CompilerParams(vmem_limit_bytes=58 * 1024 * 1024)
VM = pl.BlockSpec(memory_space=pltpu.VMEM)
SM = pl.BlockSpec(memory_space=pltpu.SMEM)


def lane_ids(rows):
    return lax.broadcasted_iota(jnp.int32, (rows, LANES), 1)


def keep_edges(units, row, r, rows):
    unit = lax.rem(r // 16, 4)
    base = lax.rem(r, 16) * 8
    lane = lane_ids(rows)
    near = jnp.logical_and(lane >= base, lane < base + 8)
    pltpu.store(units.at[unit, pl.ds(0, rows)], pltpu.roll(row, base + 4, 1), mask=near)


def pack_strips(units, west_out, east_out):
    rows = west_out.shape[1]
    low = lax.rem(lane_ids(rows), 8) < 4
    for i in range(2):
        first, second = units[2 * i], units[2 * i + 1]
        west_out[i] = jnp.where(low, pltpu.roll(second, LANES - 4, 1), first)
        east_out[i] = jnp.where(low, first, pltpu.roll(second, 4, 1))


def turn_kernel(state_ref, rows_ref, west_ref, east_ref, units):
    count = rows_ref.shape[0]
    full = CH // 8 * 8

    def body(i, _):
        for k in range(4):
            y = i * 4 + k
            rows_ref[y, 0:full] = state_ref[pl.ds(y, full, stride=count), :]
            rows_ref[y, full:CH] = state_ref[pl.ds(full * count + y, CH - full, stride=count), :]
            rows_ref[y, CH:CM] = jnp.zeros((CM - CH, LANES), jnp.float32)
            keep_edges(units, rows_ref[y], y + H, CM)
        return 0

    lax.fori_loop(0, count // 4, body, 0)
    pack_strips(units, west_ref, east_ref)


def edge_kernel(rows_ref, west_ref, east_ref, units):
    count, rows = rows_ref.shape[0], rows_ref.shape[1]

    def body(i, _):
        for k in range(4):
            keep_edges(units, rows_ref[i * 4 + k], i * 4 + k + H, rows)
        return 0

    lax.fori_loop(0, count // 4, body, 0)
    pack_strips(units, west_ref, east_ref)


def split(x):
    high = x.astype(jnp.bfloat16)
    return high, (x - high.astype(jnp.float32)).astype(jnp.bfloat16)


def mix_pair(mix_ref, first, second):
    h0, l0 = split(first)
    h1, l1 = split(second)
    high = jnp.concatenate([h0, h1], axis=1)
    low = jnp.concatenate([l0, l1], axis=1)
    stack = jnp.concatenate([high, high, low], axis=0)
    return jnp.dot(mix_ref[...], stack, preferred_element_type=jnp.float32)


CHUNK = 40


def steps_kernel(
    last, info_ref, rows_hbm, pads_ref, west_ref, east_ref, north_ref, south_ref, top_hbm, mix_ref, diff_ref,
    out_ref, a_ref, b_ref, sa_ref, sb_ref, edge_ref, wa_ref, wb_ref, fold_ref, lhs_ref, sem,
):
    count = rows_hbm.shape[0]
    tiles = wa_ref.shape[0]
    is_fold = info_ref[0] == 1
    own = info_ref[1]
    copy = pltpu.make_async_copy(rows_hbm, a_ref.at[pl.ds(H, count), pl.ds(0, CM)], sem.at[0])
    copy.start()

    @pl.when(is_fold)
    def _():
        tops = pltpu.make_async_copy(top_hbm, wa_ref.at[:, pl.ds(0, H)], sem.at[1])
        tops.start()
        tops.wait()
        for j in range(tiles):
            source = wa_ref[j, H - 1, FOLD : FOLD + 1, :]
            for block in range(tiles):
                at = (lax.broadcasted_iota(jnp.int32, (LANES, LANES), 0) + block * LANES).astype(jnp.float32)
                hit = jnp.where(at == source, 1.0, 0.0).astype(jnp.bfloat16)
                fold_ref[block * LANES : (block + 1) * LANES, j * LANES : (j + 1) * LANES] = hit

    lane = lane_ids(CP)
    low = lax.rem(lane, 8) < 4
    for i in range(2):
        fw, fe = west_ref[i], east_ref[i]
        sa_ref[2 * i] = jnp.where(low, fw, fe)
        sa_ref[2 * i + 1] = jnp.where(low, pltpu.roll(fw, LANES - 4, 1), pltpu.roll(fe, 4, 1))
    wrapped = sa_ref[0]
    sa_ref[0] = jnp.where(lane < 8 * H, south_ref[H], wrapped)
    sa_ref[4] = jnp.where(lane < 8 * H, wrapped, jnp.where(lane < 16 * H, north_ref[H], 0.0))
    edge_ref[...] = jnp.zeros(edge_ref.shape, jnp.float32)
    for k in range(H):
        a_ref[k] = south_ref[k]
        a_ref[count + H + k] = north_ref[k]
    b_ref[0] = jnp.zeros((CP, LANES), jnp.float32)
    b_ref[count + 2 * H - 1] = jnp.zeros((CP, LANES), jnp.float32)

    def set_pads(y, _):
        a_ref[y + H, CM:CP] = pads_ref[y]
        return 0

    copy.wait()
    lax.fori_loop(0, count, set_pads, 0, unroll=8)

    part_lane = lane_ids(CHUNK)
    chunks = [(c, slice(c, c + CHUNK)) for c in range(0, CP, CHUNK)]

    def fold_part(step, src, strip, w_src, w_dst):
        for j in range(tiles):
            high, below = split(w_src[j, H - 1])
            lhs_ref[0:CP, j * LANES : (j + 1) * LANES] = high
            lhs_ref[CP : 2 * CP, j * LANES : (j + 1) * LANES] = below
        for p in range(tiles // 2):
            both = jnp.dot(
                lhs_ref[...], fold_ref[:, 2 * p * LANES : 2 * (p + 1) * LANES], preferred_element_type=jnp.float32
            )
            both = both[0:CP] + both[CP : 2 * CP]
            w_src[2 * p, H] = both[:, 0:LANES]
            w_src[2 * p + 1, H] = both[:, LANES : 2 * LANES]
        src[count + H] = w_src[own, H]
        before, after = w_src[lax.rem(own + tiles - 1, tiles), H], w_src[lax.rem(own + 1, tiles), H]
        base = 8 * ((count + H) % 16)
        beside = jnp.where(low, pltpu.roll(before, base + 4, 1), pltpu.roll(after, base + 4, 1))
        strip[4] = jnp.where(jnp.logical_and(lane >= base, lane < base + 8), beside, strip[4])
        if step == NSTEP - 1:
            return

        def pair(i, _):
            k = step + 1 + i // (tiles // 2)
            j = lax.rem(i, tiles // 2) * 2
            mixed = mix_pair(mix_ref, w_src[j, k], w_src[j + 1, k])
            for m in range(2):
                here = j + m
                mask = w_src[here, k, MASK : MASK + 1, :]
                left, right = lax.rem(here + tiles - 1, tiles), lax.rem(here + 1, tiles)
                for _, ch in chunks:
                    c = w_src[here, k, ch]
                    a = jnp.where(part_lane == LANES - 1, w_src[left, k, ch], c)
                    b = jnp.where(part_lane == 0, w_src[right, k, ch], c)
                    total = pltpu.roll(a, 1, 1) + pltpu.roll(b, LANES - 1, 1)
                    total = total + (w_src[here, k - 1, ch] + w_src[here, k + 1, ch])
                    change = diff_ref[ch] * total + mixed[ch, m * LANES : (m + 1) * LANES]
                    w_dst[here, k, ch] = c + mask * change
            return 0

        lax.fori_loop(0, (H - 1 - step) * (tiles // 2), pair, 0)

    def main_part(step, src, dst, strip):
        ends = step == NSTEP - 1
        unroll = 4 if ends else 5
        first = H if ends else 1

        def body(i, _):
            start = first + i * (2 * unroll)
            mixed = [mix_pair(mix_ref, src[start + 2 * p], src[start + 2 * p + 1]) for p in range(unroll)]
            for q in range(2 * unroll):
                r = start + q
                unit = r // 16
                base = lax.rem(r, 16) * 8
                mask = src[r, MASK : MASK + 1, :]
                near = jnp.logical_and(part_lane >= base, part_lane < base + 8)
                for c0, ch in chunks:
                    c = src[r, ch]
                    beside = pltpu.roll(strip[unit, ch], LANES - 4 - base, 1)
                    a = jnp.where(part_lane == LANES - 1, beside, c)
                    b = jnp.where(part_lane == 0, beside, c)
                    total = pltpu.roll(a, 1, 1) + pltpu.roll(b, LANES - 1, 1)
                    total = total + (src[r - 1, ch] + src[r + 1, ch])
                    change = diff_ref[ch] * total + mixed[q // 2][ch, (q % 2) * LANES : (q % 2 + 1) * LANES]
                    new = c + mask * change
                    if not ends:
                        dst[r, ch] = new
                        pltpu.store(edge_ref.at[unit, pl.ds(c0, CHUNK)], pltpu.roll(c, base + 4, 1), mask=near)
                    elif last:
                        size = min(CHUNK, CH - c0)
                        out_ref[pl.ds(c0 * count + r - H, size, stride=count), :] = new[0:size]
                    else:
                        size = min(CHUNK, CM - c0)
                        out_ref[r - H, c0 : c0 + size] = new[0:size]
            return 0

        lax.fori_loop(0, (count if ends else count + 2 * H - 2) // (2 * unroll), body, 0)

    def strip_part(strip, strip_new):
        for u0, u1 in ((0, 1), (2, 3), (4, 4)):
            mixed = mix_pair(mix_ref, strip[u0], strip[u1])
            for m, u in enumerate((u0, u1) if u0 != u1 else (u0,)):
                mask = strip[u, MASK : MASK + 1, :]
                above, under = min(u + 1, 4), max(u - 1, 0)
                place = lax.rem(part_lane, 8)
                for _, ch in chunks:
                    c = strip[u, ch]
                    edges = edge_ref[u, ch]
                    a = jnp.where(place == 4, edges, c)
                    b = jnp.where(place == 3, edges, c)
                    total = pltpu.roll(a, LANES - 1, 1) + pltpu.roll(b, 1, 1)
                    n = pltpu.roll(jnp.where(part_lane < 8, strip[above, ch], c), LANES - 8, 1)
                    s = pltpu.roll(jnp.where(part_lane >= LANES - 8, strip[under, ch], c), 8, 1)
                    change = diff_ref[ch] * (total + (n + s)) + mixed[ch, m * LANES : (m + 1) * LANES]
                    strip_new[u, ch] = c + mask * change

    for step in range(NSTEP):
        even = step % 2 == 0
        src, dst = (a_ref, b_ref) if even else (b_ref, a_ref)
        strip, strip_new = (sa_ref, sb_ref) if even else (sb_ref, sa_ref)
        w_src, w_dst = (wa_ref, wb_ref) if even else (wb_ref, wa_ref)
        pl.when(is_fold)(functools.partial(fold_part, step, src, strip, w_src, w_dst))
        main_part(step, src, dst, strip)
        if step < NSTEP - 1:
            strip_part(strip, strip_new)


def f32(*shape):
    return jax.ShapeDtypeStruct(shape, jnp.float32)


def shift(x, axis, by, closed):
    count = lax.axis_size(axis)
    pairs = [(i, (i + by) % count) for i in range(count) if closed or 0 <= i + by < count]
    return lax.ppermute(x, axis, pairs)


def per_device(state, diffusivity, mixing, ocean_mask, flux_dest, flux_target, flux_weight, fold_source):
    _, channels, row_count, col_count = state.shape
    levels = channels // 2
    tx_count = lax.axis_size("tx")
    is_ocean = lax.axis_index("comp") == 1
    northmost = lax.axis_index("ty") == lax.axis_size("ty") - 1
    tile_count = lax.axis_size("ty") * tx_count
    slots = max(2, 2 * row_count // tile_count)
    info = jnp.stack([jnp.logical_and(is_ocean, northmost).astype(jnp.int32), lax.axis_index("tx").astype(jnp.int32)])

    diffuse = diffusivity[0]
    service = jnp.where(is_ocean, flux_gain, relaxation_speed)
    own_surface = jnp.where(is_ocean, 0.0, relaxation_speed)
    ids = jnp.arange(channels)
    surface_row = jnp.logical_or(ids == 0, ids == levels)
    centre = 4.0 * diffuse + jnp.where(surface_row, own_surface, 0.0)
    matrix = mix_gain * mixing[0] - jnp.where(ids[:, None] == ids[None, :], centre[:, None], 0.0)
    matrix = jnp.pad(matrix, ((0, CP - channels), (0, CP - channels)))
    at_row = lax.broadcasted_iota(jnp.int32, (CP, CP), 0)
    at_col = lax.broadcasted_iota(jnp.int32, (CP, CP), 1)
    forced = jnp.logical_or(
        jnp.logical_and(at_row == 0, at_col == FORCE), jnp.logical_and(at_row == levels, at_col == FORCE + 1)
    )
    matrix = jnp.where(forced, service, matrix)
    high = lax.reduce_precision(matrix, 8, 7)
    rest = (matrix - high).astype(jnp.bfloat16)
    high = high.astype(jnp.bfloat16)
    mix = jnp.concatenate([high, rest, high], axis=1)
    diff = jnp.broadcast_to(jnp.pad(diffuse, (0, CP - channels))[:, None], (CP, LANES))

    dest_tile = flux_dest[0, :, 0]
    target = flux_target[0]
    tile_hit = (dest_tile[:, None] == jnp.arange(tile_count, dtype=jnp.int32)[None, :]).astype(jnp.int32)
    slot_rank = jnp.sum(tile_hit * (jnp.cumsum(tile_hit, axis=0) - 1), axis=1)
    picker = (dest_tile * slots + slot_rank)[None, :] == jnp.arange(tile_count * slots, dtype=jnp.int32)[:, None]
    out_ids = jnp.sum(jnp.where(picker, target[None, :] + 1, 0), axis=1) - 1
    in_ids = lax.all_to_all(out_ids.reshape(tile_count, slots), ("ty", "tx"), split_axis=0, concat_axis=0, tiled=True)
    place = (in_ids.reshape(-1)[None, :] == jnp.arange(row_count, dtype=jnp.int32)[:, None]).astype(jnp.float32)
    pick = picker.astype(jnp.float32)
    send_mat = jnp.where(is_ocean, pick * flux_weight[0][None, :], place.T)
    take_mat = jnp.where(is_ocean, place, pick.T)

    sea_mask = jnp.where(is_ocean, ocean_mask.astype(jnp.float32), 1.0)
    fold_rows = jnp.broadcast_to(fold_source.astype(jnp.float32)[None, :], sea_mask.shape)
    blank = jnp.zeros_like(sea_mask)
    best = lax.Precision.HIGHEST

    rows = None
    for interval in range(INTERVALS):
        if interval == 0:
            surface = jnp.concatenate([state[0, 0], state[0, levels]], axis=1)
            rows, west, east = pl.pallas_call(
                turn_kernel,
                out_shape=(f32(row_count, CM, LANES), f32(2, CM, LANES), f32(2, CM, LANES)),
                in_specs=[VM],
                out_specs=(VM, VM, VM),
                scratch_shapes=[pltpu.VMEM((4, CM, LANES), jnp.float32)],
                compiler_params=PARAMS,
                name="turn",
            )(state.reshape(channels * row_count, col_count))
        else:
            surface = jnp.concatenate([rows[:, 0], rows[:, levels]], axis=1)
            west, east = pl.pallas_call(
                edge_kernel,
                out_shape=(f32(2, CM, LANES), f32(2, CM, LANES)),
                in_specs=[VM],
                out_specs=(VM, VM),
                scratch_shapes=[pltpu.VMEM((4, CM, LANES), jnp.float32)],
                compiler_params=PARAMS,
                name="edges",
            )(rows)
        other = shift(surface, "comp", 1, True)
        outgoing = jnp.dot(send_mat, other, precision=best).reshape(tile_count, slots, 2 * col_count)
        arrived = lax.all_to_all(outgoing, ("ty", "tx"), split_axis=0, concat_axis=0, tiled=True)
        force = jnp.dot(take_mat, arrived.reshape(tile_count * slots, 2 * col_count), precision=best)
        pads = jnp.stack(
            [sea_mask, fold_rows, force[:, :col_count], force[:, col_count:], blank, blank, blank, blank], axis=1
        )
        pad_west, pad_east = pl.pallas_call(
            edge_kernel,
            out_shape=(f32(2, CP - CM, LANES), f32(2, CP - CM, LANES)),
            in_specs=[VM],
            out_specs=(VM, VM),
            scratch_shapes=[pltpu.VMEM((4, CP - CM, LANES), jnp.float32)],
            compiler_params=PARAMS,
            name="pad_edges",
        )(pads)
        bottom = jnp.concatenate([rows[:H], pads[:H]], axis=1)
        top = jnp.concatenate([rows[row_count - H :], pads[row_count - H :]], axis=1)
        tops = lax.all_gather(top, "tx", axis=0, tiled=False)
        from_east = shift(jnp.concatenate([west, pad_west], axis=1), "tx", -1, True)
        from_west = shift(jnp.concatenate([east, pad_east], axis=1), "tx", 1, True)
        low = lax.broadcasted_iota(jnp.int32, (CP, LANES), 1) % 8 < 4
        strip = jnp.where(low, from_west[0], from_east[0])[None]
        from_south = shift(jnp.concatenate([top, strip], axis=0), "ty", 1, False)
        from_north = shift(jnp.concatenate([bottom, strip], axis=0), "ty", -1, False)
        last = interval == INTERVALS - 1
        rows = pl.pallas_call(
            functools.partial(steps_kernel, last),
            out_shape=f32(channels * row_count, col_count) if last else f32(row_count, CM, LANES),
            in_specs=[SM, pl.BlockSpec(memory_space=pl.ANY), VM, VM, VM, VM, VM, pl.BlockSpec(memory_space=pl.ANY), VM, VM],
            out_specs=VM,
            scratch_shapes=[
                pltpu.VMEM((row_count + 2 * H, CP, LANES), jnp.float32),
                pltpu.VMEM((row_count + 2 * H, CP, LANES), jnp.float32),
                pltpu.VMEM((5, CP, LANES), jnp.float32),
                pltpu.VMEM((5, CP, LANES), jnp.float32),
                pltpu.VMEM((5, CP, LANES), jnp.float32),
                pltpu.VMEM((tx_count, H + 1, CP, LANES), jnp.float32),
                pltpu.VMEM((tx_count, H + 1, CP, LANES), jnp.float32),
                pltpu.VMEM((tx_count * LANES, tx_count * LANES), jnp.bfloat16),
                pltpu.VMEM((2 * CP, tx_count * LANES), jnp.bfloat16),
                pltpu.SemaphoreType.DMA((2,)),
            ],
            compiler_params=PARAMS,
            name="steps",
        )(info, rows, pads, from_west, from_east, from_north, from_south, tops, mix, diff)
    return rows.reshape(1, channels, row_count, col_count)


def solution(mesh):
    in_specs = (
        P("comp", None, "ty", "tx"),
        P("comp", None),
        P("comp", None, None),
        P("ty", "tx"),
        P("tx", "ty", None),
        P("tx", "ty"),
        P("tx", "ty"),
        P("tx"),
    )
    out_specs = P("comp", None, "ty", "tx")
    return jax.shard_map(per_device, mesh=mesh, in_specs=in_specs, out_specs=out_specs, check_vma=False)
```

```python
import functools

import jax
import jax.numpy as jnp
from jax import lax
from jax.experimental import pallas as pl
from jax.experimental.pallas import tpu as pltpu
from jax.sharding import PartitionSpec as P

NSTEP = 4
INTERVALS = 2
H = NSTEP
LANES = 128
CH = 150
CM = 152
CP = 160
MASK, FOLD, FORCE = 152, 153, 154

relaxation_speed = 0.3
flux_gain = 0.25
mix_gain = 0.1

PARAMS = pltpu.CompilerParams(vmem_limit_bytes=58 * 1024 * 1024)
VM = pl.BlockSpec(memory_space=pltpu.VMEM)
ANY = pl.BlockSpec(memory_space=pl.ANY)
SM = pl.BlockSpec(memory_space=pltpu.SMEM)


def lane_ids(rows):
    return lax.broadcasted_iota(jnp.int32, (rows, LANES), 1)


def keep_edges(units, row, group, k, rows):
    unit = lax.rem(group + (k + H) // 16, 4)
    base = (k + H) % 16 * 8
    lane = lane_ids(rows)
    near = jnp.logical_and(lane >= base, lane < base + 8)
    pltpu.store(units.at[unit, pl.ds(0, rows)], pltpu.roll(row, (base + 4) % LANES, 1), mask=near)


def pack_strips(units, west_out, east_out):
    rows = west_out.shape[1]
    low = lax.rem(lane_ids(rows), 8) < 4
    for i in range(2):
        first, second = units[2 * i], units[2 * i + 1]
        west_out[i] = jnp.where(low, pltpu.roll(second, LANES - 4, 1), first)
        east_out[i] = jnp.where(low, first, pltpu.roll(second, 4, 1))


def turn_kernel(state_ref, rows_ref, west_ref, east_ref, units):
    count = rows_ref.shape[0]
    full = CH // 8 * 8

    def body(i, _):
        for k in range(16):
            y = i * 16 + k
            rows_ref[y, 0:full] = state_ref[pl.ds(y, full, stride=count), :]
            rows_ref[y, full:CH] = state_ref[pl.ds(full * count + y, CH - full, stride=count), :]
            rows_ref[y, CH:CM] = jnp.zeros((CM - CH, LANES), jnp.float32)
        for k in range(16):
            keep_edges(units, rows_ref[i * 16 + k], i, k, CM)
        return 0

    lax.fori_loop(0, count // 16, body, 0)
    pack_strips(units, west_ref, east_ref)


def edge_kernel(rows_ref, west_ref, east_ref, units):
    count, rows = rows_ref.shape[0], rows_ref.shape[1]

    def body(i, _):
        for k in range(16):
            keep_edges(units, rows_ref[i * 16 + k], i, k, rows)
        return 0

    lax.fori_loop(0, count // 16, body, 0)
    pack_strips(units, west_ref, east_ref)


def split(x):
    high = x.astype(jnp.bfloat16)
    return high, (x - high.astype(jnp.float32)).astype(jnp.bfloat16)


def mix_pair(mix_ref, first, second):
    h0, l0 = split(first)
    h1, l1 = split(second)
    high = jnp.concatenate([h0, h1], axis=1)
    low = jnp.concatenate([l0, l1], axis=1)
    stack = jnp.concatenate([high, high, low], axis=0)
    return jnp.dot(mix_ref[...], stack, preferred_element_type=jnp.float32)


CHUNK = 40
CHUNKS = [(c, slice(c, c + CHUNK)) for c in range(0, CP, CHUNK)]


def update_rows(spots, src, ext, mix_ref, diff_ref, put, put_ext):
    lane = lane_ids(CHUNK)
    mixed = [mix_pair(mix_ref, src[spot[0]], ext[spot[0]]) for spot in spots]
    for (here, under, above), both in zip(spots, mixed):
        mask = src[here, MASK : MASK + 1, :]
        mask_ext = ext[here, MASK : MASK + 1, :]
        for c0, ch in CHUNKS:
            c, e = src[here, ch], ext[here, ch]
            total = pltpu.roll(jnp.where(lane == LANES - 1, e, c), 1, 1)
            total = total + pltpu.roll(jnp.where(lane == 0, e, c), LANES - 1, 1)
            total = total + (src[under, ch] + src[above, ch])
            put(here, c0, c + mask * (diff_ref[ch] * total + both[ch, 0:LANES]))
            if put_ext is None:
                continue
            total = pltpu.roll(jnp.where(lane == LANES - 1, c, e), 1, 1)
            total = total + pltpu.roll(jnp.where(lane == 0, c, e), LANES - 1, 1)
            total = total + (ext[under, ch] + ext[above, ch])
            put_ext(here, c0, e + mask_ext * (diff_ref[ch] * total + both[ch, LANES : 2 * LANES]))


UNROLL = 10


def inner_kernel(
    last, rows_hbm, pads_ref, west_ref, east_ref, mix_ref, diff_ref,
    out_ref, sides_ref, near_ref, a_ref, b_ref, ea_ref, eb_ref, strip_ref, sem,
):
    count = rows_hbm.shape[0]
    copy = pltpu.make_async_copy(rows_hbm, a_ref.at[:, pl.ds(0, CM)], sem.at[0])
    copy.start()
    lane = lane_ids(CP)
    low = lax.rem(lane, 8) < 4
    for i in range(2):
        fw, fe = west_ref[i], east_ref[i]
        strip_ref[2 * i] = jnp.where(low, fw, fe)
        strip_ref[2 * i + 1] = jnp.where(low, pltpu.roll(fw, LANES - 4, 1), pltpu.roll(fe, 4, 1))

    def spread(i, _):
        for k in range(16):
            unit = lax.rem(i + (k + H) // 16, 4)
            ea_ref[i * 16 + k] = pltpu.roll(strip_ref[unit], LANES - 4 - (k + H) % 16 * 8, 1)
        return 0

    lax.fori_loop(0, count // 16, spread, 0)
    copy.wait()

    def set_pads(y, _):
        a_ref[y, CM:CP] = pads_ref[y]
        return 0

    lax.fori_loop(0, count, set_pads, 0, unroll=8)
    for step in range(NSTEP):
        even = step % 2 == 0
        src, dst = (a_ref, b_ref) if even else (b_ref, a_ref)
        ext, ext_dst = (ea_ref, eb_ref) if even else (eb_ref, ea_ref)
        ends = step == NSTEP - 1
        for k in range(2):
            sides_ref[step, 0, k, 0] = src[step + k]
            sides_ref[step, 0, k, 1] = ext[step + k]
            sides_ref[step, 1, k, 0] = src[count - 1 - step - k]
            sides_ref[step, 1, k, 1] = ext[count - 1 - step - k]

        def put(y, c0, value):
            if not ends:
                dst[y, c0 : c0 + CHUNK] = value
            elif last:
                size = min(CHUNK, CH - c0)
                out_ref[pl.ds(c0 * count + y, size, stride=count), :] = value[0:size]
            else:
                size = min(CHUNK, CM - c0)
                out_ref[y, c0 : c0 + size] = value[0:size]

        def put_ext(y, c0, value):
            ext_dst[y, c0 : c0 + CHUNK] = value

        first, number = step + 1, count - 2 * step - 2

        def some(start, amount):
            spots = [(start + q, start + q - 1, start + q + 1) for q in range(amount)]
            update_rows(spots, src, ext, mix_ref, diff_ref, put, None if ends else put_ext)

        def body(i, _):
            some(first + i * UNROLL, UNROLL)
            return 0

        lax.fori_loop(0, number // UNROLL, body, 0)
        if number % UNROLL:
            some(first + number // UNROLL * UNROLL, number % UNROLL)
    if last:
        for k in range(H):
            near_ref[0, k] = out_ref[pl.ds(H + k, CH, stride=count), :]
            near_ref[1, k] = out_ref[pl.ds(count - 1 - H - k, CH, stride=count), :]


def outer_kernel(
    last, info_ref, sides_ref, near_ref, north_ref, south_ref, folds_ref, mix_ref, diff_ref, rows_hbm,
    out_hbm, a_ref, b_ref, ea_ref, eb_ref, done_ref, sem,
):
    is_fold = info_ref[0] == 1
    for k in range(H):
        a_ref[0, k] = south_ref[k]
        a_ref[1, H - 1 - k] = north_ref[k]
        ea_ref[0, k] = pltpu.roll(south_ref[H], (LANES - 4 - 8 * k) % LANES, 1)
        ea_ref[1, H - 1 - k] = pltpu.roll(north_ref[H], LANES - 4 - 8 * (H + k), 1)
    for step in range(NSTEP):
        even = step % 2 == 0
        src, dst = (a_ref, b_ref) if even else (b_ref, a_ref)
        ext, ext_dst = (ea_ref, eb_ref) if even else (eb_ref, ea_ref)
        for side in range(2):
            for k in range(2):
                src[side, H + step + k] = sides_ref[step, side, k, 0]
                ext[side, H + step + k] = sides_ref[step, side, k, 1]

        @pl.when(is_fold)
        def _():
            src[1, H - 1] = folds_ref[step, 0]
            ext[1, H - 1] = folds_ref[step, 1]

        ends = step == NSTEP - 1

        def put(spot, c0, value):
            side, k = spot
            if not ends:
                dst[side, k, c0 : c0 + CHUNK] = value
            elif last:
                y = k - H if side == 0 else 7 - (k - H)
                size = min(CHUNK, CH - c0)
                done_ref[side, pl.ds(c0 * 8 + y, size, stride=8), :] = value[0:size]
            else:
                y = k - H if side == 0 else H - 1 - (k - H)
                size = min(CHUNK, CM - c0)
                done_ref[side, y, c0 : c0 + size] = value[0:size]

        def put_ext(spot, c0, value):
            side, k = spot
            ext_dst[side, k, c0 : c0 + CHUNK] = value

        spots = [((m, k), (m, k - 1), (m, k + 1)) for m in range(2) for k in range(step + 1, step + 1 + H)]
        update_rows(spots, At(src), At(ext), mix_ref, diff_ref, put, None if ends else put_ext)
    if last:
        count = out_hbm.shape[1]
        for k in range(H):
            done_ref[0, pl.ds(H + k, CH, stride=8), :] = near_ref[0, k]
            done_ref[1, pl.ds(H - 1 - k, CH, stride=8), :] = near_ref[1, k]
        copies = [
            pltpu.make_async_copy(done_ref.at[m].reshape(CH, 8, LANES), out_hbm.at[:, pl.ds(at, 8)], sem.at[m])
            for m, at in ((0, 0), (1, count - 8))
        ]
    else:
        count = out_hbm.shape[0]
        copies = [
            pltpu.make_async_copy(done_ref.at[m], out_hbm.at[pl.ds(at, H)], sem.at[m]) for m, at in ((0, 0), (1, count - H))
        ]
    for copy in copies:
        copy.start()
    for copy in copies:
        copy.wait()


class At:
    def __init__(self, ref):
        self.ref = ref

    def __getitem__(self, key):
        if isinstance(key[0], tuple):
            return self.ref[(*key[0], *key[1:])]
        return self.ref[key]


def fold_kernel(info_ref, top_hbm, mix_ref, diff_ref, out_ref, wa_ref, wb_ref, fold_ref, lhs_ref, sem):
    tiles = wa_ref.shape[0]
    own = info_ref[1]

    @pl.when(info_ref[0] == 1)
    def _():
        tops = pltpu.make_async_copy(top_hbm, wa_ref.at[:, pl.ds(0, H)], sem.at[0])
        tops.start()
        tops.wait()
        for j in range(tiles):
            source = wa_ref[j, H - 1, FOLD : FOLD + 1, :]
            for block in range(tiles):
                at = (lax.broadcasted_iota(jnp.int32, (LANES, LANES), 0) + block * LANES).astype(jnp.float32)
                hit = jnp.where(at == source, 1.0, 0.0).astype(jnp.bfloat16)
                fold_ref[block * LANES : (block + 1) * LANES, j * LANES : (j + 1) * LANES] = hit
        lane = lane_ids(CP)
        part_lane = lane_ids(CHUNK)
        for step in range(NSTEP):
            w_src, w_dst = (wa_ref, wb_ref) if step % 2 == 0 else (wb_ref, wa_ref)
            for j in range(tiles):
                high, below = split(w_src[j, H - 1])
                lhs_ref[0:CP, j * LANES : (j + 1) * LANES] = high
                lhs_ref[CP : 2 * CP, j * LANES : (j + 1) * LANES] = below
            for p in range(tiles // 2):
                both = jnp.dot(
                    lhs_ref[...], fold_ref[:, 2 * p * LANES : 2 * (p + 1) * LANES], preferred_element_type=jnp.float32
                )
                both = both[0:CP] + both[CP : 2 * CP]
                w_src[2 * p, H] = both[:, 0:LANES]
                w_src[2 * p + 1, H] = both[:, LANES : 2 * LANES]
            out_ref[step, 0] = w_src[own, H]
            before, after = w_src[lax.rem(own + tiles - 1, tiles), H], w_src[lax.rem(own + 1, tiles), H]
            out_ref[step, 1] = jnp.where(lane < LANES // 2, after, before)
            if step == NSTEP - 1:
                continue

            def row(k, _):
                mixed = [mix_pair(mix_ref, w_src[j, k], w_src[j + 1, k]) for j in range(0, tiles, 2)]
                for here in range(tiles):
                    mask = w_src[here, k, MASK : MASK + 1, :]
                    left, right = (here + tiles - 1) % tiles, (here + 1) % tiles
                    m = here % 2
                    for _, ch in CHUNKS:
                        c = w_src[here, k, ch]
                        total = pltpu.roll(jnp.where(part_lane == LANES - 1, w_src[left, k, ch], c), 1, 1)
                        total = total + pltpu.roll(jnp.where(part_lane == 0, w_src[right, k, ch], c), LANES - 1, 1)
                        total = total + (w_src[here, k - 1, ch] + w_src[here, k + 1, ch])
                        change = diff_ref[ch] * total + mixed[here // 2][ch, m * LANES : (m + 1) * LANES]
                        w_dst[here, k, ch] = c + mask * change
                return 0

            lax.fori_loop(step + 1, H, row, 0)


def cost(us):
    return pl.CostEstimate(flops=int(us * 1e9), bytes_accessed=int(us * 3e6), transcendentals=0)


def f32(*shape):
    return jax.ShapeDtypeStruct(shape, jnp.float32)


def shift(x, axis, by, closed):
    count = lax.axis_size(axis)
    pairs = [(i, (i + by) % count) for i in range(count) if closed or 0 <= i + by < count]
    return lax.ppermute(x, axis, pairs)


def per_device(state, diffusivity, mixing, ocean_mask, flux_dest, flux_target, flux_weight, fold_source):
    _, channels, row_count, col_count = state.shape
    levels = channels // 2
    tx_count = lax.axis_size("tx")
    is_ocean = lax.axis_index("comp") == 1
    northmost = lax.axis_index("ty") == lax.axis_size("ty") - 1
    tile_count = lax.axis_size("ty") * tx_count
    slots = max(2, 2 * row_count // tile_count)
    info = jnp.stack([jnp.logical_and(is_ocean, northmost).astype(jnp.int32), lax.axis_index("tx").astype(jnp.int32)])

    diffuse = diffusivity[0]
    service = jnp.where(is_ocean, flux_gain, relaxation_speed)
    own_surface = jnp.where(is_ocean, 0.0, relaxation_speed)
    ids = jnp.arange(channels)
    surface_row = jnp.logical_or(ids == 0, ids == levels)
    centre = 4.0 * diffuse + jnp.where(surface_row, own_surface, 0.0)
    matrix = mix_gain * mixing[0] - jnp.where(ids[:, None] == ids[None, :], centre[:, None], 0.0)
    matrix = jnp.pad(matrix, ((0, CP - channels), (0, CP - channels)))
    at_row = lax.broadcasted_iota(jnp.int32, (CP, CP), 0)
    at_col = lax.broadcasted_iota(jnp.int32, (CP, CP), 1)
    forced = jnp.logical_or(
        jnp.logical_and(at_row == 0, at_col == FORCE), jnp.logical_and(at_row == levels, at_col == FORCE + 1)
    )
    matrix = jnp.where(forced, service, matrix)
    high = lax.reduce_precision(matrix, 8, 7)
    rest = (matrix - high).astype(jnp.bfloat16)
    high = high.astype(jnp.bfloat16)
    mix = jnp.concatenate([high, rest, high], axis=1)
    diff = jnp.broadcast_to(jnp.pad(diffuse, (0, CP - channels))[:, None], (CP, LANES))

    dest_tile = flux_dest[0, :, 0]
    target = flux_target[0]
    tile_hit = (dest_tile[:, None] == jnp.arange(tile_count, dtype=jnp.int32)[None, :]).astype(jnp.int32)
    slot_rank = jnp.sum(tile_hit * (jnp.cumsum(tile_hit, axis=0) - 1), axis=1)
    picker = (dest_tile * slots + slot_rank)[None, :] == jnp.arange(tile_count * slots, dtype=jnp.int32)[:, None]
    out_ids = jnp.sum(jnp.where(picker, target[None, :] + 1, 0), axis=1) - 1
    in_ids = lax.all_to_all(out_ids.reshape(tile_count, slots), ("ty", "tx"), split_axis=0, concat_axis=0, tiled=True)
    place = (in_ids.reshape(-1)[None, :] == jnp.arange(row_count, dtype=jnp.int32)[:, None]).astype(jnp.float32)
    pick = picker.astype(jnp.float32)
    send_mat = jnp.where(is_ocean, pick * flux_weight[0][None, :], place.T)
    take_mat = jnp.where(is_ocean, place, pick.T)

    sea_mask = jnp.where(is_ocean, ocean_mask.astype(jnp.float32), 1.0)
    fold_rows = jnp.broadcast_to(fold_source.astype(jnp.float32)[None, :], sea_mask.shape)
    blank = jnp.zeros_like(sea_mask)
    best = lax.Precision.HIGHEST

    rows = None
    for interval in range(INTERVALS):
        if interval == 0:
            surface = jnp.concatenate([state[0, 0], state[0, levels]], axis=1)
            rows, west, east = pl.pallas_call(
                turn_kernel,
                out_shape=(f32(row_count, CM, LANES), f32(2, CM, LANES), f32(2, CM, LANES)),
                in_specs=[VM],
                out_specs=(VM, VM, VM),
                scratch_shapes=[pltpu.VMEM((4, CM, LANES), jnp.float32)],
                compiler_params=PARAMS,
                cost_estimate=cost(10),
            name="turn",
            )(state.reshape(channels * row_count, col_count))
        else:
            surface = jnp.concatenate([rows[:, 0], rows[:, levels]], axis=1)
            west, east = pl.pallas_call(
                edge_kernel,
                out_shape=(f32(2, CM, LANES), f32(2, CM, LANES)),
                in_specs=[VM],
                out_specs=(VM, VM),
                scratch_shapes=[pltpu.VMEM((4, CM, LANES), jnp.float32)],
                compiler_params=PARAMS,
                cost_estimate=cost(5),
            name="edges",
            )(rows)
        other = shift(surface, "comp", 1, True)
        outgoing = jnp.dot(send_mat, other, precision=best).reshape(tile_count, slots, 2 * col_count)
        arrived = lax.all_to_all(outgoing, ("ty", "tx"), split_axis=0, concat_axis=0, tiled=True)
        force = jnp.dot(take_mat, arrived.reshape(tile_count * slots, 2 * col_count), precision=best)
        pads = jnp.stack(
            [sea_mask, fold_rows, force[:, :col_count], force[:, col_count:], blank, blank, blank, blank], axis=1
        )
        pad_west, pad_east = pl.pallas_call(
            edge_kernel,
            out_shape=(f32(2, CP - CM, LANES), f32(2, CP - CM, LANES)),
            in_specs=[VM],
            out_specs=(VM, VM),
            scratch_shapes=[pltpu.VMEM((4, CP - CM, LANES), jnp.float32)],
            compiler_params=PARAMS,
            cost_estimate=cost(2),
            name="pad_edges",
        )(pads)
        bottom = jnp.concatenate([rows[:H], pads[:H]], axis=1)
        top = jnp.concatenate([rows[row_count - H :], pads[row_count - H :]], axis=1)
        tops = lax.all_gather(top, "tx", axis=0, tiled=False)
        from_east = shift(jnp.concatenate([west, pad_west], axis=1), "tx", -1, True)
        from_west = shift(jnp.concatenate([east, pad_east], axis=1), "tx", 1, True)
        low = lax.broadcasted_iota(jnp.int32, (CP, LANES), 1) % 8 < 4
        strip = jnp.where(low, from_west[0], from_east[0])[None]
        from_south = shift(jnp.concatenate([top, strip], axis=0), "ty", 1, False)
        from_north = shift(jnp.concatenate([bottom, strip], axis=0), "ty", -1, False)
        last = interval == INTERVALS - 1
        tile_buffer = pltpu.VMEM((row_count, CP, LANES), jnp.float32)
        inner, sides, near = pl.pallas_call(
            functools.partial(inner_kernel, last),
            out_shape=(
                f32(channels * row_count, col_count) if last else f32(row_count, CM, LANES),
                f32(NSTEP, 2, 2, 2, CP, LANES),
                f32(2, H, CH, LANES),
            ),
            in_specs=[ANY, VM, VM, VM, VM, VM],
            out_specs=(VM, VM, VM),
            scratch_shapes=[tile_buffer] * 4 + [pltpu.VMEM((4, CP, LANES), jnp.float32), pltpu.SemaphoreType.DMA((1,))],
            compiler_params=PARAMS,
            cost_estimate=cost(30),
            name="inner",
        )(rows, pads, from_west, from_east, mix, diff)
        wide = pltpu.VMEM((tx_count, H + 1, CP, LANES), jnp.float32)
        folds = pl.pallas_call(
            fold_kernel,
            out_shape=f32(NSTEP, 2, CP, LANES),
            in_specs=[SM, ANY, VM, VM],
            out_specs=VM,
            scratch_shapes=[
                wide,
                wide,
                pltpu.VMEM((tx_count * LANES, tx_count * LANES), jnp.bfloat16),
                pltpu.VMEM((2 * CP, tx_count * LANES), jnp.bfloat16),
                pltpu.SemaphoreType.DMA((1,)),
            ],
            compiler_params=PARAMS,
            cost_estimate=cost(10),
            name="fold",
        )(info, tops, mix, diff)
        side_buffer = pltpu.VMEM((2, 2 * H + 2, CP, LANES), jnp.float32)
        if last:
            inner = inner.reshape(channels, row_count, col_count)
            done = pltpu.VMEM((2, channels * 8, LANES), jnp.float32)
        else:
            done = pltpu.VMEM((2, H, CM, LANES), jnp.float32)
        rows = pl.pallas_call(
            functools.partial(outer_kernel, last),
            out_shape=f32(*inner.shape),
            in_specs=[SM, VM, VM, VM, VM, VM, VM, VM, ANY],
            out_specs=ANY,
            scratch_shapes=[side_buffer] * 4 + [done, pltpu.SemaphoreType.DMA((2,))],
            input_output_aliases={8: 0},
            compiler_params=PARAMS,
            cost_estimate=cost(5),
            name="outer",
        )(info, sides, near, from_north, from_south, folds, mix, diff, inner)
    return rows.reshape(1, channels, row_count, col_count)


def solution(mesh):
    in_specs = (
        P("comp", None, "ty", "tx"),
        P("comp", None),
        P("comp", None, None),
        P("ty", "tx"),
        P("tx", "ty", None),
        P("tx", "ty"),
        P("tx", "ty"),
        P("tx"),
    )
    out_specs = P("comp", None, "ty", "tx")
    return jax.shard_map(per_device, mesh=mesh, in_specs=in_specs, out_specs=out_specs, check_vma=False)
```

```python
import functools

import jax
import jax.numpy as jnp
from jax import lax
from jax.experimental import pallas as pl
from jax.experimental.pallas import tpu as pltpu
from jax.sharding import PartitionSpec as P

NSTEP = 4
INTERVALS = 2
H = NSTEP
LANES = 128
CH = 150
CM = 152
CP = 160
MASK, FOLD, FORCE = 152, 153, 154

relaxation_speed = 0.3
flux_gain = 0.25
mix_gain = 0.1

PARAMS = pltpu.CompilerParams(vmem_limit_bytes=58 * 1024 * 1024)
VM = pl.BlockSpec(memory_space=pltpu.VMEM)
ANY = pl.BlockSpec(memory_space=pl.ANY)
SM = pl.BlockSpec(memory_space=pltpu.SMEM)


def lane_ids(rows):
    return lax.broadcasted_iota(jnp.int32, (rows, LANES), 1)


def keep_edges(units, value, unit, base, c0):
    rows = value.shape[0]
    lane = lane_ids(rows)
    near = jnp.logical_and(lane >= base, lane < base + 8)
    pltpu.store(units.at[unit, pl.ds(c0, rows)], pltpu.roll(value, (base + 4) % LANES, 1), mask=near)


def lanes_of(y):
    return (y + H) // 16 % 4, (y + H) % 16 * 8


def pack_strips(units, west_out, east_out):
    rows = west_out.shape[1]
    low = lax.rem(lane_ids(rows), 8) < 4
    for i in range(2):
        first, second = units[2 * i], units[2 * i + 1]
        west_out[i] = jnp.where(low, pltpu.roll(second, LANES - 4, 1), first)
        east_out[i] = jnp.where(low, first, pltpu.roll(second, 4, 1))


ROWS = 16


def turn_kernel(state_ref, rows_ref, west_ref, east_ref, units):
    full = CH // 8 * 8
    step = pl.program_id(0)
    flat = state_ref.reshape(CH * ROWS, LANES)
    for k in range(ROWS):
        rows_ref[k, 0:full] = flat[pl.ds(k, full, stride=ROWS), :]
        rows_ref[k, full:CH] = flat[pl.ds(full * ROWS + k, CH - full, stride=ROWS), :]
        rows_ref[k, CH:CM] = jnp.zeros((CM - CH, LANES), jnp.float32)
    for k in range(ROWS):
        keep_edges(units, rows_ref[k], lax.rem(step + (k + H) // ROWS, 4), lanes_of(k)[1], 0)

    @pl.when(step == pl.num_programs(0) - 1)
    def _():
        pack_strips(units, west_ref, east_ref)


def edge_kernel(rows_ref, west_ref, east_ref, units):
    step = pl.program_id(0)
    for k in range(ROWS):
        keep_edges(units, rows_ref[k], lax.rem(step + (k + H) // ROWS, 4), lanes_of(k)[1], 0)

    @pl.when(step == pl.num_programs(0) - 1)
    def _():
        pack_strips(units, west_ref, east_ref)


def pad_kernel(pads_ref, west_ref, east_ref, rows_hbm, west_out, east_out, bottom_ref, top_ref, units, pw_ref, pe_ref, sem):
    count = pads_ref.shape[0]
    copies = [
        pltpu.make_async_copy(rows_hbm.at[pl.ds(at, H)], to.at[:, pl.ds(0, CM)], sem.at[m])
        for m, (at, to) in enumerate(((0, bottom_ref), (count - H, top_ref)))
    ]
    for copy in copies:
        copy.start()
    for y in range(count):
        keep_edges(units, pads_ref[y], *lanes_of(y), 0)
    pack_strips(units, pw_ref, pe_ref)
    west_out[:, 0:CM], west_out[:, CM:CP] = west_ref[...], pw_ref[...]
    east_out[:, 0:CM], east_out[:, CM:CP] = east_ref[...], pe_ref[...]
    for copy in copies:
        copy.wait()
    bottom_ref[:, CM:CP], top_ref[:, CM:CP] = pads_ref[0:H], pads_ref[count - H : count]


def plan_kernel(dest_ref, target_ref, pick_ref, ids_ref):
    tiles, count = ids_ref.shape[0], dest_ref.shape[1]
    hit = lax.broadcasted_iota(jnp.int32, (tiles, count), 0) == dest_ref[...]
    before = lax.broadcasted_iota(jnp.int32, (count, count), 0) < lax.broadcasted_iota(jnp.int32, (count, count), 1)
    ones = jnp.where(hit, 1.0, 0.0)
    rank = jnp.dot(ones, jnp.where(before, 1.0, 0.0), preferred_element_type=jnp.float32)
    wanted = (target_ref[...] + 1).astype(jnp.float32)
    found = []
    for k in range(2):
        pick = jnp.where(jnp.abs(rank - k) < 0.5, ones, 0.0)
        pick_ref[pl.ds(k, tiles, stride=2), :] = pick
        found.append(jnp.sum(pick * wanted, axis=1, keepdims=True) - 1.0)
    ids_ref[...] = jnp.concatenate(found, axis=1).astype(jnp.int32)


def split(x):
    high = x.astype(jnp.bfloat16)
    return high, (x - high.astype(jnp.float32)).astype(jnp.bfloat16)


def mix_pair(mix_ref, first, second):
    h0, l0 = split(first)
    h1, l1 = split(second)
    high = jnp.concatenate([h0, h1], axis=1)
    low = jnp.concatenate([l0, l1], axis=1)
    stack = jnp.concatenate([high, high, low], axis=0)
    return jnp.dot(mix_ref[...], stack, preferred_element_type=jnp.float32)


CHUNK = 40
CHUNKS = [(c, slice(c, min(c + CHUNK, CM))) for c in range(0, CM, CHUNK)]
SERVICE = slice(CM, CP)


def update_rows(spots, src, ext, mix_ref, diff_ref, put, put_ext):
    mixed = [mix_pair(mix_ref, src[spot[0]], ext[spot[0]]) for spot in spots]
    for (here, under, above), both in zip(spots, mixed):
        mask = src[here, MASK : MASK + 1, :]
        mask_ext = ext[here, MASK : MASK + 1, :]
        for c0, ch in CHUNKS:
            c, e = src[here, ch], ext[here, ch]
            lane = lane_ids(c.shape[0])
            total = pltpu.roll(jnp.where(lane == LANES - 1, e, c), 1, 1)
            total = total + pltpu.roll(jnp.where(lane == 0, e, c), LANES - 1, 1)
            total = total + (src[under, ch] + src[above, ch])
            put(here, c0, c + mask * (diff_ref[ch] * total + both[ch, 0:LANES]))
            if put_ext is None:
                continue
            total = pltpu.roll(jnp.where(lane == LANES - 1, c, e), 1, 1)
            total = total + pltpu.roll(jnp.where(lane == 0, c, e), LANES - 1, 1)
            total = total + (ext[under, ch] + ext[above, ch])
            put_ext(here, c0, e + mask_ext * (diff_ref[ch] * total + both[ch, LANES : 2 * LANES]))


def inner_kernel(
    last, rows_hbm, pads_ref, west_ref, east_ref, mix_ref, diff_ref,
    out_ref, sides_ref, near_ref, a_ref, b_ref, ea_ref, eb_ref, strip_ref, sem,
):
    count = rows_hbm.shape[0]
    copy = pltpu.make_async_copy(rows_hbm, a_ref.at[:, pl.ds(0, CM)], sem.at[0])
    copy.start()
    lane = lane_ids(CP)
    low = lax.rem(lane, 8) < 4
    for i in range(2):
        fw, fe = west_ref[i], east_ref[i]
        strip_ref[2 * i] = jnp.where(low, fw, fe)
        strip_ref[2 * i + 1] = jnp.where(low, pltpu.roll(fw, LANES - 4, 1), pltpu.roll(fe, 4, 1))

    def spread(i, _):
        for k in range(16):
            unit = lax.rem(i + (k + H) // 16, 4)
            beside = pltpu.roll(strip_ref[unit], LANES - 4 - (k + H) % 16 * 8, 1)
            ea_ref[i * 16 + k] = beside
            eb_ref[i * 16 + k, SERVICE] = beside[SERVICE]
        return 0

    lax.fori_loop(0, count // 16, spread, 0)
    copy.wait()

    def set_pads(y, _):
        a_ref[y, CM:CP] = pads_ref[y]
        b_ref[y, CM:CP] = pads_ref[y]
        return 0

    lax.fori_loop(0, count, set_pads, 0, unroll=8)
    for step in range(NSTEP):
        even = step % 2 == 0
        src, dst = (a_ref, b_ref) if even else (b_ref, a_ref)
        ext, ext_dst = (ea_ref, eb_ref) if even else (eb_ref, ea_ref)
        ends = step == NSTEP - 1
        for k in range(2):
            sides_ref[step, 0, k, 0] = src[step + k]
            sides_ref[step, 0, k, 1] = ext[step + k]
            sides_ref[step, 1, k, 0] = src[count - 1 - step - k]
            sides_ref[step, 1, k, 1] = ext[count - 1 - step - k]

        def put(y, c0, value):
            if not ends:
                dst[y, c0 : c0 + value.shape[0]] = value
            elif last:
                size = min(CHUNK, CH - c0)
                out_ref[pl.ds(c0 * count + y, size, stride=count), :] = value[0:size]
            else:
                size = min(CHUNK, CM - c0)
                out_ref[y, c0 : c0 + size] = value[0:size]

        def put_ext(y, c0, value):
            ext_dst[y, c0 : c0 + value.shape[0]] = value

        first, number = step + 1, count - 2 * step - 2

        def some(start, amount):
            spots = [(start + q, start + q - 1, start + q + 1) for q in range(amount)]
            update_rows(spots, src, ext, mix_ref, diff_ref, put, None if ends else put_ext)

        half = number // 2

        def body(i, _):
            some(first + i * half, half)
            return 0

        lax.fori_loop(0, 2, body, 0)
    if last:
        for k in range(H):
            near_ref[0, k] = out_ref[pl.ds(H + k, CH, stride=count), :]
            near_ref[1, k] = out_ref[pl.ds(count - 1 - H - k, CH, stride=count), :]


def outer_kernel(
    last, info_ref, sides_ref, near_ref, north_ref, south_ref, folds_ref, mix_ref, diff_ref, rows_hbm,
    out_hbm, a_ref, b_ref, ea_ref, eb_ref, done_ref, sem,
):
    is_fold = info_ref[0] == 1
    for k in range(H):
        a_ref[0, k] = south_ref[k]
        a_ref[1, H - 1 - k] = north_ref[k]
        ea_ref[0, k] = pltpu.roll(south_ref[H], (LANES - 4 - 8 * k) % LANES, 1)
        ea_ref[1, H - 1 - k] = pltpu.roll(north_ref[H], LANES - 4 - 8 * (H + k), 1)
        for side in range(2):
            b_ref[side, k, SERVICE] = a_ref[side, k, SERVICE]
            eb_ref[side, k, SERVICE] = ea_ref[side, k, SERVICE]
    for step in range(NSTEP):
        even = step % 2 == 0
        src, dst = (a_ref, b_ref) if even else (b_ref, a_ref)
        ext, ext_dst = (ea_ref, eb_ref) if even else (eb_ref, ea_ref)
        for side in range(2):
            for k in range(2):
                src[side, H + step + k] = sides_ref[step, side, k, 0]
                ext[side, H + step + k] = sides_ref[step, side, k, 1]
            dst[side, H + step, SERVICE] = sides_ref[step, side, 0, 0, SERVICE]
            ext_dst[side, H + step, SERVICE] = sides_ref[step, side, 0, 1, SERVICE]

        @pl.when(is_fold)
        def _():
            src[1, H - 1] = folds_ref[step, 0]
            ext[1, H - 1] = folds_ref[step, 1]

        ends = step == NSTEP - 1

        def put(spot, c0, value):
            side, k = spot
            if not ends:
                dst[side, k, c0 : c0 + value.shape[0]] = value
            elif last:
                y = k - H if side == 0 else 7 - (k - H)
                size = min(CHUNK, CH - c0)
                done_ref[side, pl.ds(c0 * 8 + y, size, stride=8), :] = value[0:size]
            else:
                y = k - H if side == 0 else H - 1 - (k - H)
                size = min(CHUNK, CM - c0)
                done_ref[side, y, c0 : c0 + size] = value[0:size]

        def put_ext(spot, c0, value):
            side, k = spot
            ext_dst[side, k, c0 : c0 + value.shape[0]] = value

        spots = [((m, k), (m, k - 1), (m, k + 1)) for m in range(2) for k in range(step + 1, step + 1 + H)]
        update_rows(spots, At(src), At(ext), mix_ref, diff_ref, put, None if ends else put_ext)
    if last:
        count = out_hbm.shape[1]
        for k in range(H):
            done_ref[0, pl.ds(H + k, CH, stride=8), :] = near_ref[0, k]
            done_ref[1, pl.ds(H - 1 - k, CH, stride=8), :] = near_ref[1, k]
        copies = [
            pltpu.make_async_copy(done_ref.at[m].reshape(CH, 8, LANES), out_hbm.at[:, pl.ds(at, 8)], sem.at[m])
            for m, at in ((0, 0), (1, count - 8))
        ]
    else:
        count = out_hbm.shape[0]
        copies = [
            pltpu.make_async_copy(done_ref.at[m], out_hbm.at[pl.ds(at, H)], sem.at[m]) for m, at in ((0, 0), (1, count - H))
        ]
    for copy in copies:
        copy.start()
    for copy in copies:
        copy.wait()


class At:
    def __init__(self, ref):
        self.ref = ref

    def __getitem__(self, key):
        if isinstance(key[0], tuple):
            return self.ref[(*key[0], *key[1:])]
        return self.ref[key]


def fold_kernel(info_ref, top_hbm, mix_ref, diff_ref, out_ref, wa_ref, wb_ref, fold_ref, lhs_ref, sem):
    tiles = wa_ref.shape[0]
    own = info_ref[1]

    @pl.when(info_ref[0] == 1)
    def _():
        tops = pltpu.make_async_copy(top_hbm, wa_ref.at[:, pl.ds(0, H)], sem.at[0])
        service = pltpu.make_async_copy(
            top_hbm.at[:, :, pl.ds(CM, CP - CM)], wb_ref.at[:, pl.ds(0, H), pl.ds(CM, CP - CM)], sem.at[1]
        )
        tops.start()
        service.start()
        tops.wait()
        service.wait()
        for j in range(tiles):
            source = wa_ref[j, H - 1, FOLD : FOLD + 1, :]
            for block in range(tiles):
                at = (lax.broadcasted_iota(jnp.int32, (LANES, LANES), 0) + block * LANES).astype(jnp.float32)
                hit = jnp.where(at == source, 1.0, 0.0).astype(jnp.bfloat16)
                fold_ref[block * LANES : (block + 1) * LANES, j * LANES : (j + 1) * LANES] = hit
        lane = lane_ids(CP)
        for step in range(NSTEP):
            w_src, w_dst = (wa_ref, wb_ref) if step % 2 == 0 else (wb_ref, wa_ref)
            for j in range(tiles):
                high, below = split(w_src[j, H - 1])
                lhs_ref[0:CP, j * LANES : (j + 1) * LANES] = high
                lhs_ref[CP : 2 * CP, j * LANES : (j + 1) * LANES] = below
            for p in range(tiles // 2):
                both = jnp.dot(
                    lhs_ref[...], fold_ref[:, 2 * p * LANES : 2 * (p + 1) * LANES], preferred_element_type=jnp.float32
                )
                both = both[0:CP] + both[CP : 2 * CP]
                w_src[2 * p, H] = both[:, 0:LANES]
                w_src[2 * p + 1, H] = both[:, LANES : 2 * LANES]
            out_ref[step, 0] = w_src[own, H]
            before, after = w_src[lax.rem(own + tiles - 1, tiles), H], w_src[lax.rem(own + 1, tiles), H]
            out_ref[step, 1] = jnp.where(lane < LANES // 2, after, before)
            if step == NSTEP - 1:
                continue

            def row(k, _):
                mixed = [mix_pair(mix_ref, w_src[j, k], w_src[j + 1, k]) for j in range(0, tiles, 2)]
                for here in range(tiles):
                    mask = w_src[here, k, MASK : MASK + 1, :]
                    left, right = (here + tiles - 1) % tiles, (here + 1) % tiles
                    m = here % 2
                    for _, ch in CHUNKS:
                        c = w_src[here, k, ch]
                        part_lane = lane_ids(c.shape[0])
                        total = pltpu.roll(jnp.where(part_lane == LANES - 1, w_src[left, k, ch], c), 1, 1)
                        total = total + pltpu.roll(jnp.where(part_lane == 0, w_src[right, k, ch], c), LANES - 1, 1)
                        total = total + (w_src[here, k - 1, ch] + w_src[here, k + 1, ch])
                        change = diff_ref[ch] * total + mixed[here // 2][ch, m * LANES : (m + 1) * LANES]
                        w_dst[here, k, ch] = c + mask * change
                return 0

            lax.fori_loop(step + 1, H, row, 0)


def cost(us):
    return pl.CostEstimate(flops=int(us * 1e9), bytes_accessed=int(us * 3e6), transcendentals=0)


def f32(*shape):
    return jax.ShapeDtypeStruct(shape, jnp.float32)


def shift(x, axis, by, closed):
    count = lax.axis_size(axis)
    pairs = [(i, (i + by) % count) for i in range(count) if closed or 0 <= i + by < count]
    return lax.ppermute(x, axis, pairs)


def per_device(state, diffusivity, mixing, ocean_mask, flux_dest, flux_target, flux_weight, fold_source):
    _, channels, row_count, col_count = state.shape
    levels = channels // 2
    tx_count = lax.axis_size("tx")
    is_ocean = lax.axis_index("comp") == 1
    northmost = lax.axis_index("ty") == lax.axis_size("ty") - 1
    tile_count = lax.axis_size("ty") * tx_count
    slots = max(2, 2 * row_count // tile_count)
    info = jnp.stack([jnp.logical_and(is_ocean, northmost).astype(jnp.int32), lax.axis_index("tx").astype(jnp.int32)])

    diffuse = diffusivity[0]
    service = jnp.where(is_ocean, flux_gain, relaxation_speed)
    own_surface = jnp.where(is_ocean, 0.0, relaxation_speed)
    ids = jnp.arange(channels)
    surface_row = jnp.logical_or(ids == 0, ids == levels)
    centre = 4.0 * diffuse + jnp.where(surface_row, own_surface, 0.0)
    matrix = mix_gain * mixing[0] - jnp.where(ids[:, None] == ids[None, :], centre[:, None], 0.0)
    matrix = jnp.pad(matrix, ((0, CP - channels), (0, CP - channels)))
    at_row = lax.broadcasted_iota(jnp.int32, (CP, CP), 0)
    at_col = lax.broadcasted_iota(jnp.int32, (CP, CP), 1)
    forced = jnp.logical_or(
        jnp.logical_and(at_row == 0, at_col == FORCE), jnp.logical_and(at_row == levels, at_col == FORCE + 1)
    )
    matrix = jnp.where(forced, service, matrix)
    high = lax.reduce_precision(matrix, 8, 7)
    rest = (matrix - high).astype(jnp.bfloat16)
    high = high.astype(jnp.bfloat16)
    mix = jnp.concatenate([high, rest, high], axis=1)[:CM]
    diff = jnp.broadcast_to(jnp.pad(diffuse, (0, CM - channels))[:, None], (CM, LANES))

    pick, out_ids = pl.pallas_call(
        plan_kernel,
        out_shape=(f32(tile_count * slots, row_count), jax.ShapeDtypeStruct((tile_count, slots), jnp.int32)),
        in_specs=[VM, VM],
        out_specs=(VM, VM),
        compiler_params=PARAMS,
        name="plan",
    )(flux_dest[:, :, 0], flux_target)
    in_ids = lax.all_to_all(out_ids, ("ty", "tx"), split_axis=0, concat_axis=0, tiled=True)
    place = (in_ids.reshape(-1)[None, :] == jnp.arange(row_count, dtype=jnp.int32)[:, None]).astype(jnp.float32)
    here = jnp.where(is_ocean, 1.0, 0.0)
    send_mat = jnp.where(is_ocean, place.T, pick * flux_weight[0][None, :])
    send_mat = jnp.concatenate([send_mat * here, send_mat * (1.0 - here)], axis=0)
    take_mat = jnp.where(is_ocean, place, pick.T)
    take_mat = jnp.concatenate([take_mat * here, take_mat * (1.0 - here)], axis=1)
    everyone = ("comp", "ty", "tx")

    sea_mask = jnp.where(is_ocean, ocean_mask.astype(jnp.float32), 1.0)
    fold_rows = jnp.broadcast_to(fold_source.astype(jnp.float32)[None, :], sea_mask.shape)
    blank = jnp.zeros_like(sea_mask)
    best = lax.Precision.HIGHEST

    rows = None
    for interval in range(INTERVALS):
        if interval == 0:
            surface = jnp.concatenate([state[0, 0], state[0, levels]], axis=1)
            rows, west, east = pl.pallas_call(
                turn_kernel,
                grid=(row_count // ROWS,),
                out_shape=(f32(row_count, CM, LANES), f32(2, CM, LANES), f32(2, CM, LANES)),
                in_specs=[pl.BlockSpec((CH, ROWS, LANES), lambda i: (0, i, 0))],
                out_specs=(
                    pl.BlockSpec((ROWS, CM, LANES), lambda i: (i, 0, 0)),
                    pl.BlockSpec((2, CM, LANES), lambda i: (0, 0, 0)),
                    pl.BlockSpec((2, CM, LANES), lambda i: (0, 0, 0)),
                ),
                scratch_shapes=[pltpu.VMEM((4, CM, LANES), jnp.float32)],
                compiler_params=PARAMS,
                cost_estimate=cost(10),
                name="turn",
            )(state[0])
        else:
            surface = lax.optimization_barrier(jnp.concatenate([rows[:, 0], rows[:, levels]], axis=1))
            west, east = pl.pallas_call(
                edge_kernel,
                grid=(row_count // ROWS,),
                out_shape=(f32(2, CM, LANES), f32(2, CM, LANES)),
                in_specs=[pl.BlockSpec((ROWS, CM, LANES), lambda i: (i, 0, 0))],
                out_specs=(
                    pl.BlockSpec((2, CM, LANES), lambda i: (0, 0, 0)),
                    pl.BlockSpec((2, CM, LANES), lambda i: (0, 0, 0)),
                ),
                scratch_shapes=[pltpu.VMEM((4, CM, LANES), jnp.float32)],
                compiler_params=PARAMS,
                cost_estimate=cost(5),
                name="edges",
            )(rows)
        outgoing = jnp.dot(send_mat, surface, precision=best).reshape(2 * tile_count, slots, 2 * col_count)
        arrived = lax.all_to_all(outgoing, everyone, split_axis=0, concat_axis=0, tiled=True)
        arrived, west, east = lax.optimization_barrier((arrived, west, east))
        force = jnp.dot(take_mat, arrived.reshape(2 * tile_count * slots, 2 * col_count), precision=best)
        pads = jnp.stack(
            [sea_mask, fold_rows, force[:, :col_count], force[:, col_count:], blank, blank, blank, blank], axis=1
        )
        west, east, bottom, top = pl.pallas_call(
            pad_kernel,
            out_shape=(f32(2, CP, LANES), f32(2, CP, LANES), f32(H, CP, LANES), f32(H, CP, LANES)),
            in_specs=[VM, VM, VM, ANY],
            out_specs=(VM, VM, VM, VM),
            scratch_shapes=[pltpu.VMEM((4, CP - CM, LANES), jnp.float32)]
            + [pltpu.VMEM((2, CP - CM, LANES), jnp.float32)] * 2
            + [pltpu.SemaphoreType.DMA((2,))],
            compiler_params=PARAMS,
            cost_estimate=cost(2),
            name="pad_edges",
        )(pads, west, east, rows)
        tops = lax.all_gather(top, "tx", axis=0, tiled=False)
        from_east = shift(west, "tx", -1, True)
        from_west = shift(east, "tx", 1, True)
        low = lax.broadcasted_iota(jnp.int32, (CP, LANES), 1) % 8 < 4
        strip = jnp.where(low, from_west[0], from_east[0])[None]
        from_south = shift(jnp.concatenate([top, strip], axis=0), "ty", 1, False)
        from_north = shift(jnp.concatenate([bottom, strip], axis=0), "ty", -1, False)
        last = interval == INTERVALS - 1
        tile_buffer = pltpu.VMEM((row_count, CP, LANES), jnp.float32)
        inner, sides, near = pl.pallas_call(
            functools.partial(inner_kernel, last),
            out_shape=(
                f32(channels * row_count, col_count) if last else f32(row_count, CM, LANES),
                f32(NSTEP, 2, 2, 2, CP, LANES),
                f32(2, H, CH, LANES),
            ),
            in_specs=[ANY, VM, VM, VM, VM, VM],
            out_specs=(VM, VM, VM),
            scratch_shapes=[tile_buffer] * 4 + [pltpu.VMEM((4, CP, LANES), jnp.float32), pltpu.SemaphoreType.DMA((1,))],
            compiler_params=PARAMS,
            cost_estimate=cost(30),
            name="inner",
        )(rows, pads, from_west, from_east, mix, diff)
        wide = pltpu.VMEM((tx_count, H + 1, CP, LANES), jnp.float32)
        folds = pl.pallas_call(
            fold_kernel,
            out_shape=f32(NSTEP, 2, CP, LANES),
            in_specs=[SM, ANY, VM, VM],
            out_specs=VM,
            scratch_shapes=[
                wide,
                wide,
                pltpu.VMEM((tx_count * LANES, tx_count * LANES), jnp.bfloat16),
                pltpu.VMEM((2 * CP, tx_count * LANES), jnp.bfloat16),
                pltpu.SemaphoreType.DMA((2,)),
            ],
            compiler_params=PARAMS,
            cost_estimate=cost(10),
            name="fold",
        )(info, tops, mix, diff)
        side_buffer = pltpu.VMEM((2, 2 * H + 2, CP, LANES), jnp.float32)
        if last:
            inner = inner.reshape(channels, row_count, col_count)
            done = pltpu.VMEM((2, channels * 8, LANES), jnp.float32)
        else:
            done = pltpu.VMEM((2, H, CM, LANES), jnp.float32)
        rows = pl.pallas_call(
            functools.partial(outer_kernel, last),
            out_shape=f32(*inner.shape),
            in_specs=[SM, VM, VM, VM, VM, VM, VM, VM, ANY],
            out_specs=ANY,
            scratch_shapes=[side_buffer] * 4 + [done, pltpu.SemaphoreType.DMA((2,))],
            input_output_aliases={8: 0},
            compiler_params=PARAMS,
            cost_estimate=cost(5),
            name="outer",
        )(info, sides, near, from_north, from_south, folds, mix, diff, inner)
    return rows.reshape(1, channels, row_count, col_count)


def solution(mesh):
    in_specs = (
        P("comp", None, "ty", "tx"),
        P("comp", None),
        P("comp", None, None),
        P("ty", "tx"),
        P("tx", "ty", None),
        P("tx", "ty"),
        P("tx", "ty"),
        P("tx"),
    )
    out_specs = P("comp", None, "ty", "tx")
    return jax.shard_map(per_device, mesh=mesh, in_specs=in_specs, out_specs=out_specs, check_vma=False)
```

```python
import functools

import jax
import jax.numpy as jnp
from jax import lax
from jax.experimental import pallas as pl
from jax.experimental.pallas import tpu as pltpu
from jax.sharding import PartitionSpec as P

NSTEP = 4
INTERVALS = 2
H = NSTEP
LANES = 128
CH = 150
CM = 152
CP = 160
MASK, FOLD, FORCE = 152, 153, 154

relaxation_speed = 0.3
flux_gain = 0.25
mix_gain = 0.1


def params(mib):
    return pltpu.CompilerParams(vmem_limit_bytes=mib * 1024 * 1024)


VM = pl.BlockSpec(memory_space=pltpu.VMEM)
ANY = pl.BlockSpec(memory_space=pltpu.HBM)
SM = pl.BlockSpec(memory_space=pltpu.SMEM)


def lane_ids(rows):
    return lax.broadcasted_iota(jnp.int32, (rows, LANES), 1)


def keep_edges(units, value, unit, base, c0):
    rows = value.shape[0]
    lane = lane_ids(rows)
    near = jnp.logical_and(lane >= base, lane < base + 8)
    pltpu.store(units.at[unit, pl.ds(c0, rows)], pltpu.roll(value, (base + 4) % LANES, 1), mask=near)


def lanes_of(y):
    return (y + H) // 16 % 4, (y + H) % 16 * 8


def pack_strips(units, west_out, east_out):
    rows = west_out.shape[1]
    low = lax.rem(lane_ids(rows), 8) < 4
    for i in range(2):
        first, second = units[2 * i], units[2 * i + 1]
        west_out[i] = jnp.where(low, pltpu.roll(second, LANES - 4, 1), first)
        east_out[i] = jnp.where(low, first, pltpu.roll(second, 4, 1))


ROWS = 16


def turn_kernel(state_ref, rows_ref, west_ref, east_ref, units):
    full = CH // 8 * 8
    step = pl.program_id(0)
    flat = state_ref.reshape(CH * ROWS, LANES)
    for k in range(ROWS):
        rows_ref[k, 0:full] = flat[pl.ds(k, full, stride=ROWS), :]
        rows_ref[k, full:CH] = flat[pl.ds(full * ROWS + k, CH - full, stride=ROWS), :]
        rows_ref[k, CH:CM] = jnp.zeros((CM - CH, LANES), jnp.float32)
    for k in range(ROWS):
        keep_edges(units, rows_ref[k], lax.rem(step + (k + H) // ROWS, 4), lanes_of(k)[1], 0)

    @pl.when(step == pl.num_programs(0) - 1)
    def _():
        pack_strips(units, west_ref, east_ref)


def edge_kernel(rows_ref, west_ref, east_ref, units):
    step = pl.program_id(0)
    for k in range(ROWS):
        keep_edges(units, rows_ref[k], lax.rem(step + (k + H) // ROWS, 4), lanes_of(k)[1], 0)

    @pl.when(step == pl.num_programs(0) - 1)
    def _():
        pack_strips(units, west_ref, east_ref)


def pad_kernel(pads_ref, west_ref, east_ref, rows_hbm, west_out, east_out, bottom_ref, top_ref, units, pw_ref, pe_ref, sem):
    count = pads_ref.shape[0]
    copies = [
        pltpu.make_async_copy(rows_hbm.at[pl.ds(at, H)], to.at[:, pl.ds(0, CM)], sem.at[m])
        for m, (at, to) in enumerate(((0, bottom_ref), (count - H, top_ref)))
    ]
    for copy in copies:
        copy.start()
    for y in range(count):
        keep_edges(units, pads_ref[y], *lanes_of(y), 0)
    pack_strips(units, pw_ref, pe_ref)
    west_out[:, 0:CM], west_out[:, CM:CP] = west_ref[...], pw_ref[...]
    east_out[:, 0:CM], east_out[:, CM:CP] = east_ref[...], pe_ref[...]
    for copy in copies:
        copy.wait()
    bottom_ref[:, CM:CP], top_ref[:, CM:CP] = pads_ref[0:H], pads_ref[count - H : count]


def plan_kernel(dest_ref, target_ref, pick_ref, ids_ref):
    tiles, count = ids_ref.shape[0], dest_ref.shape[1]
    hit = lax.broadcasted_iota(jnp.int32, (tiles, count), 0) == dest_ref[...]
    before = lax.broadcasted_iota(jnp.int32, (count, count), 0) < lax.broadcasted_iota(jnp.int32, (count, count), 1)
    ones = jnp.where(hit, 1.0, 0.0)
    rank = jnp.dot(ones, jnp.where(before, 1.0, 0.0), preferred_element_type=jnp.float32)
    wanted = (target_ref[...] + 1).astype(jnp.float32)
    found = []
    for k in range(2):
        pick = jnp.where(jnp.abs(rank - k) < 0.5, ones, 0.0)
        pick_ref[pl.ds(k, tiles, stride=2), :] = pick
        found.append(jnp.sum(pick * wanted, axis=1, keepdims=True) - 1.0)
    ids_ref[...] = jnp.concatenate(found, axis=1).astype(jnp.int32)


def split(x):
    high = x.astype(jnp.bfloat16)
    return high, (x - high.astype(jnp.float32)).astype(jnp.bfloat16)


def mix_pair(mix_ref, first, second):
    h0, l0 = split(first)
    h1, l1 = split(second)
    high = jnp.concatenate([h0, h1], axis=1)
    low = jnp.concatenate([l0, l1], axis=1)
    stack = jnp.concatenate([high, high, low], axis=0)
    return jnp.dot(mix_ref[...], stack, preferred_element_type=jnp.float32)


CHUNK = 40
CHUNKS = [(c, slice(c, min(c + CHUNK, CM))) for c in range(0, CM, CHUNK)]
SERVICE = slice(CM, CP)


def update_rows(spots, src, ext, mix_ref, diff_ref, put, put_ext):
    mixed = [mix_pair(mix_ref, src[spot[0]], ext[spot[0]]) for spot in spots]
    for (here, under, above), both in zip(spots, mixed):
        mask = src[here, MASK : MASK + 1, :]
        mask_ext = ext[here, MASK : MASK + 1, :]
        for c0, ch in CHUNKS:
            c, e = src[here, ch], ext[here, ch]
            lane = lane_ids(c.shape[0])
            total = pltpu.roll(jnp.where(lane == LANES - 1, e, c), 1, 1)
            total = total + pltpu.roll(jnp.where(lane == 0, e, c), LANES - 1, 1)
            total = total + (src[under, ch] + src[above, ch])
            put(here, c0, c + mask * (diff_ref[ch] * total + both[ch, 0:LANES]))
            if put_ext is None:
                continue
            total = pltpu.roll(jnp.where(lane == LANES - 1, c, e), 1, 1)
            total = total + pltpu.roll(jnp.where(lane == 0, c, e), LANES - 1, 1)
            total = total + (ext[under, ch] + ext[above, ch])
            put_ext(here, c0, e + mask_ext * (diff_ref[ch] * total + both[ch, LANES : 2 * LANES]))


def inner_kernel(
    last, rows_hbm, pads_ref, west_ref, east_ref, mix_ref, diff_ref,
    out_hbm, sides_ref, near_ref, a_ref, b_ref, ea_ref, eb_ref, strip_ref, out_ref, sem,
):
    count = rows_hbm.shape[0]
    copy = pltpu.make_async_copy(rows_hbm, a_ref.at[:, pl.ds(0, CM)], sem.at[0])
    copy.start()
    lane = lane_ids(CP)
    low = lax.rem(lane, 8) < 4
    for i in range(2):
        fw, fe = west_ref[i], east_ref[i]
        strip_ref[2 * i] = jnp.where(low, fw, fe)
        strip_ref[2 * i + 1] = jnp.where(low, pltpu.roll(fw, LANES - 4, 1), pltpu.roll(fe, 4, 1))

    def spread(i, _):
        for k in range(16):
            unit = lax.rem(i + (k + H) // 16, 4)
            beside = pltpu.roll(strip_ref[unit], LANES - 4 - (k + H) % 16 * 8, 1)
            ea_ref[i * 16 + k] = beside
            eb_ref[i * 16 + k, SERVICE] = beside[SERVICE]
        return 0

    lax.fori_loop(0, count // 16, spread, 0)
    copy.wait()

    def set_pads(y, _):
        a_ref[y, CM:CP] = pads_ref[y]
        b_ref[y, CM:CP] = pads_ref[y]
        return 0

    lax.fori_loop(0, count, set_pads, 0, unroll=8)
    for step in range(NSTEP):
        even = step % 2 == 0
        src, dst = (a_ref, b_ref) if even else (b_ref, a_ref)
        ext, ext_dst = (ea_ref, eb_ref) if even else (eb_ref, ea_ref)
        ends = step == NSTEP - 1
        for k in range(2):
            sides_ref[step, 0, k, 0] = src[step + k]
            sides_ref[step, 0, k, 1] = ext[step + k]
            sides_ref[step, 1, k, 0] = src[count - 1 - step - k]
            sides_ref[step, 1, k, 1] = ext[count - 1 - step - k]

        def put(y, c0, value):
            if ends and last:
                size = min(CHUNK, CH - c0)
                out_ref[pl.ds(c0 * count + y, size, stride=count), :] = value[0:size]
            else:
                dst[y, c0 : c0 + value.shape[0]] = value

        def put_ext(y, c0, value):
            ext_dst[y, c0 : c0 + value.shape[0]] = value

        first, number = step + 1, count - 2 * step - 2

        def some(start, amount):
            spots = [(start + q, start + q - 1, start + q + 1) for q in range(amount)]
            update_rows(spots, src, ext, mix_ref, diff_ref, put, None if ends else put_ext)

        half = number // 2

        def result(i):
            if last:
                block = pl.ds(pl.multiple_of(2 * H + i * (half - H), 8), half - H)
                return pltpu.make_async_copy(
                    out_ref.reshape(CH, count, LANES).at[:, block], out_hbm.at[:, block], sem.at[i]
                )
            block = pl.ds(first + i * half, half)
            return pltpu.make_async_copy(dst.at[block, pl.ds(0, CM)], out_hbm.at[block], sem.at[i])


        def body(i, _):
            some(first + i * half, half)
            if ends:
                result(i).start()
            return 0

        lax.fori_loop(0, 2, body, 0)
    if last:
        for k in range(H):
            near_ref[0, k] = out_ref[pl.ds(H + k, CH, stride=count), :]
            near_ref[1, k] = out_ref[pl.ds(count - 1 - H - k, CH, stride=count), :]
    for i in range(2):
        result(i).wait()


def outer_kernel(
    last, info_ref, sides_ref, near_ref, north_ref, south_ref, folds_ref, mix_ref, diff_ref, rows_hbm,
    out_hbm, a_ref, b_ref, ea_ref, eb_ref, done_ref, sem,
):
    is_fold = info_ref[0] == 1
    for k in range(H):
        a_ref[0, k] = south_ref[k]
        a_ref[1, H - 1 - k] = north_ref[k]
        ea_ref[0, k] = pltpu.roll(south_ref[H], (LANES - 4 - 8 * k) % LANES, 1)
        ea_ref[1, H - 1 - k] = pltpu.roll(north_ref[H], LANES - 4 - 8 * (H + k), 1)
        for side in range(2):
            b_ref[side, k, SERVICE] = a_ref[side, k, SERVICE]
            eb_ref[side, k, SERVICE] = ea_ref[side, k, SERVICE]
    for step in range(NSTEP):
        even = step % 2 == 0
        src, dst = (a_ref, b_ref) if even else (b_ref, a_ref)
        ext, ext_dst = (ea_ref, eb_ref) if even else (eb_ref, ea_ref)
        for side in range(2):
            for k in range(2):
                src[side, H + step + k] = sides_ref[step, side, k, 0]
                ext[side, H + step + k] = sides_ref[step, side, k, 1]
            dst[side, H + step, SERVICE] = sides_ref[step, side, 0, 0, SERVICE]
            ext_dst[side, H + step, SERVICE] = sides_ref[step, side, 0, 1, SERVICE]

        @pl.when(is_fold)
        def _():
            src[1, H - 1] = folds_ref[step, 0]
            ext[1, H - 1] = folds_ref[step, 1]

        ends = step == NSTEP - 1

        def put(spot, c0, value):
            side, k = spot
            if not ends:
                dst[side, k, c0 : c0 + value.shape[0]] = value
            elif last:
                y = k - H if side == 0 else 7 - (k - H)
                size = min(CHUNK, CH - c0)
                done_ref[side, pl.ds(c0 * 8 + y, size, stride=8), :] = value[0:size]
            else:
                y = k - H if side == 0 else H - 1 - (k - H)
                size = min(CHUNK, CM - c0)
                done_ref[side, y, c0 : c0 + size] = value[0:size]

        def put_ext(spot, c0, value):
            side, k = spot
            ext_dst[side, k, c0 : c0 + value.shape[0]] = value

        spots = [((m, k), (m, k - 1), (m, k + 1)) for m in range(2) for k in range(step + 1, step + 1 + H)]
        update_rows(spots, At(src), At(ext), mix_ref, diff_ref, put, None if ends else put_ext)
    if last:
        count = out_hbm.shape[1]
        for k in range(H):
            done_ref[0, pl.ds(H + k, CH, stride=8), :] = near_ref[0, k]
            done_ref[1, pl.ds(H - 1 - k, CH, stride=8), :] = near_ref[1, k]
        copies = [
            pltpu.make_async_copy(done_ref.at[m].reshape(CH, 8, LANES), out_hbm.at[:, pl.ds(at, 8)], sem.at[m])
            for m, at in ((0, 0), (1, count - 8))
        ]
    else:
        count = out_hbm.shape[0]
        copies = [
            pltpu.make_async_copy(done_ref.at[m], out_hbm.at[pl.ds(at, H)], sem.at[m]) for m, at in ((0, 0), (1, count - H))
        ]
    for copy in copies:
        copy.start()
    for copy in copies:
        copy.wait()


class At:
    def __init__(self, ref):
        self.ref = ref

    def __getitem__(self, key):
        if isinstance(key[0], tuple):
            return self.ref[(*key[0], *key[1:])]
        return self.ref[key]


def fold_kernel(info_ref, top_hbm, mix_ref, diff_ref, out_ref, wa_ref, wb_ref, fold_ref, lhs_ref, sem):
    tiles = wa_ref.shape[0]
    own = info_ref[1]

    @pl.when(info_ref[0] == 1)
    def _():
        tops = pltpu.make_async_copy(top_hbm, wa_ref.at[:, pl.ds(0, H)], sem.at[0])
        service = pltpu.make_async_copy(
            top_hbm.at[:, :, pl.ds(CM, CP - CM)], wb_ref.at[:, pl.ds(0, H), pl.ds(CM, CP - CM)], sem.at[1]
        )
        tops.start()
        service.start()
        tops.wait()
        service.wait()
        for j in range(tiles):
            source = wa_ref[j, H - 1, FOLD : FOLD + 1, :]
            for block in range(tiles):
                at = (lax.broadcasted_iota(jnp.int32, (LANES, LANES), 0) + block * LANES).astype(jnp.float32)
                hit = jnp.where(at == source, 1.0, 0.0).astype(jnp.bfloat16)
                fold_ref[block * LANES : (block + 1) * LANES, j * LANES : (j + 1) * LANES] = hit
        lane = lane_ids(CP)
        for step in range(NSTEP):
            w_src, w_dst = (wa_ref, wb_ref) if step % 2 == 0 else (wb_ref, wa_ref)
            for j in range(tiles):
                high, below = split(w_src[j, H - 1])
                lhs_ref[0:CP, j * LANES : (j + 1) * LANES] = high
                lhs_ref[CP : 2 * CP, j * LANES : (j + 1) * LANES] = below
            for p in range(tiles // 2):
                both = jnp.dot(
                    lhs_ref[...], fold_ref[:, 2 * p * LANES : 2 * (p + 1) * LANES], preferred_element_type=jnp.float32
                )
                both = both[0:CP] + both[CP : 2 * CP]
                w_src[2 * p, H] = both[:, 0:LANES]
                w_src[2 * p + 1, H] = both[:, LANES : 2 * LANES]
            out_ref[step, 0] = w_src[own, H]
            before, after = w_src[lax.rem(own + tiles - 1, tiles), H], w_src[lax.rem(own + 1, tiles), H]
            out_ref[step, 1] = jnp.where(lane < LANES // 2, after, before)
            if step == NSTEP - 1:
                continue

            for k in range(step + 1, H):
                mixed = [mix_pair(mix_ref, w_src[j, k], w_src[j + 1, k]) for j in range(0, tiles, 2)]
                for here in range(tiles):
                    mask = w_src[here, k, MASK : MASK + 1, :]
                    left, right = (here + tiles - 1) % tiles, (here + 1) % tiles
                    m = here % 2
                    for _, ch in CHUNKS:
                        c = w_src[here, k, ch]
                        part_lane = lane_ids(c.shape[0])
                        total = pltpu.roll(jnp.where(part_lane == LANES - 1, w_src[left, k, ch], c), 1, 1)
                        total = total + pltpu.roll(jnp.where(part_lane == 0, w_src[right, k, ch], c), LANES - 1, 1)
                        total = total + (w_src[here, k - 1, ch] + w_src[here, k + 1, ch])
                        change = diff_ref[ch] * total + mixed[here // 2][ch, m * LANES : (m + 1) * LANES]
                        w_dst[here, k, ch] = c + mask * change


def cost(us):
    return pl.CostEstimate(flops=int(us * 1e9), bytes_accessed=int(us * 3e6), transcendentals=0)


def f32(*shape):
    return jax.ShapeDtypeStruct(shape, jnp.float32)


def shift(x, axis, by, closed):
    count = lax.axis_size(axis)
    pairs = [(i, (i + by) % count) for i in range(count) if closed or 0 <= i + by < count]
    return lax.ppermute(x, axis, pairs)


def per_device(state, diffusivity, mixing, ocean_mask, flux_dest, flux_target, flux_weight, fold_source):
    _, channels, row_count, col_count = state.shape
    levels = channels // 2
    tx_count = lax.axis_size("tx")
    is_ocean = lax.axis_index("comp") == 1
    northmost = lax.axis_index("ty") == lax.axis_size("ty") - 1
    tile_count = lax.axis_size("ty") * tx_count
    slots = max(2, 2 * row_count // tile_count)
    info = jnp.stack([jnp.logical_and(is_ocean, northmost).astype(jnp.int32), lax.axis_index("tx").astype(jnp.int32)])

    diffuse = diffusivity[0]
    service = jnp.where(is_ocean, flux_gain, relaxation_speed)
    own_surface = jnp.where(is_ocean, 0.0, relaxation_speed)
    ids = jnp.arange(channels)
    surface_row = jnp.logical_or(ids == 0, ids == levels)
    centre = 4.0 * diffuse + jnp.where(surface_row, own_surface, 0.0)
    matrix = mix_gain * mixing[0] - jnp.where(ids[:, None] == ids[None, :], centre[:, None], 0.0)
    matrix = jnp.pad(matrix, ((0, CP - channels), (0, CP - channels)))
    at_row = lax.broadcasted_iota(jnp.int32, (CP, CP), 0)
    at_col = lax.broadcasted_iota(jnp.int32, (CP, CP), 1)
    forced = jnp.logical_or(
        jnp.logical_and(at_row == 0, at_col == FORCE), jnp.logical_and(at_row == levels, at_col == FORCE + 1)
    )
    matrix = jnp.where(forced, service, matrix)
    high = lax.reduce_precision(matrix, 8, 7)
    rest = (matrix - high).astype(jnp.bfloat16)
    high = high.astype(jnp.bfloat16)
    mix = jnp.concatenate([high, rest, high], axis=1)[:CM]
    diff = jnp.broadcast_to(jnp.pad(diffuse, (0, CM - channels))[:, None], (CM, LANES))

    pick, out_ids = pl.pallas_call(
        plan_kernel,
        out_shape=(f32(tile_count * slots, row_count), jax.ShapeDtypeStruct((tile_count, slots), jnp.int32)),
        in_specs=[VM, VM],
        out_specs=(VM, VM),
        compiler_params=params(57),
        name="plan",
    )(flux_dest[:, :, 0], flux_target)
    in_ids = lax.all_to_all(out_ids, ("ty", "tx"), split_axis=0, concat_axis=0, tiled=True)
    place = (in_ids.reshape(-1)[None, :] == jnp.arange(row_count, dtype=jnp.int32)[:, None]).astype(jnp.float32)
    here = jnp.where(is_ocean, 1.0, 0.0)
    send_mat = jnp.where(is_ocean, place.T, pick * flux_weight[0][None, :])
    send_mat = jnp.concatenate([send_mat * here, send_mat * (1.0 - here)], axis=0)
    take_mat = jnp.where(is_ocean, place, pick.T)
    take_mat = jnp.concatenate([take_mat * here, take_mat * (1.0 - here)], axis=1)
    everyone = ("comp", "ty", "tx")

    sea_mask = jnp.where(is_ocean, ocean_mask.astype(jnp.float32), 1.0)
    fold_rows = jnp.broadcast_to(fold_source.astype(jnp.float32)[None, :], sea_mask.shape)
    blank = jnp.zeros_like(sea_mask)
    best = lax.Precision.HIGHEST

    rows = None
    for interval in range(INTERVALS):
        if interval == 0:
            surface = jnp.concatenate([state[0, 0], state[0, levels]], axis=1)
            rows, west, east = pl.pallas_call(
                turn_kernel,
                grid=(row_count // ROWS,),
                out_shape=(f32(row_count, CM, LANES), f32(2, CM, LANES), f32(2, CM, LANES)),
                in_specs=[pl.BlockSpec((CH, ROWS, LANES), lambda i: (0, i, 0))],
                out_specs=(
                    pl.BlockSpec((ROWS, CM, LANES), lambda i: (i, 0, 0)),
                    pl.BlockSpec((2, CM, LANES), lambda i: (0, 0, 0)),
                    pl.BlockSpec((2, CM, LANES), lambda i: (0, 0, 0)),
                ),
                scratch_shapes=[pltpu.VMEM((4, CM, LANES), jnp.float32)],
                compiler_params=params(58),
                cost_estimate=cost(10),
                name="turn",
            )(state[0])
        else:
            surface = lax.optimization_barrier(jnp.concatenate([rows[:, 0], rows[:, levels]], axis=1))
            west, east = pl.pallas_call(
                edge_kernel,
                grid=(row_count // ROWS,),
                out_shape=(f32(2, CM, LANES), f32(2, CM, LANES)),
                in_specs=[pl.BlockSpec((ROWS, CM, LANES), lambda i: (i, 0, 0))],
                out_specs=(
                    pl.BlockSpec((2, CM, LANES), lambda i: (0, 0, 0)),
                    pl.BlockSpec((2, CM, LANES), lambda i: (0, 0, 0)),
                ),
                scratch_shapes=[pltpu.VMEM((4, CM, LANES), jnp.float32)],
                compiler_params=params(58),
                cost_estimate=cost(5),
                name="edges",
            )(rows)
        outgoing = jnp.dot(send_mat, surface, precision=best).reshape(2 * tile_count, slots, 2 * col_count)
        arrived = lax.all_to_all(outgoing, everyone, split_axis=0, concat_axis=0, tiled=True)
        arrived, west, east, mix, diff, info = lax.optimization_barrier((arrived, west, east, mix, diff, info))
        force = jnp.dot(take_mat, arrived.reshape(2 * tile_count * slots, 2 * col_count), precision=best)
        pads = jnp.stack(
            [sea_mask, fold_rows, force[:, :col_count], force[:, col_count:], blank, blank, blank, blank], axis=1
        )
        west, east, bottom, top = pl.pallas_call(
            pad_kernel,
            out_shape=(f32(2, CP, LANES), f32(2, CP, LANES), f32(H, CP, LANES), f32(H, CP, LANES)),
            in_specs=[VM, VM, VM, ANY],
            out_specs=(VM, VM, VM, VM),
            scratch_shapes=[pltpu.VMEM((4, CP - CM, LANES), jnp.float32)]
            + [pltpu.VMEM((2, CP - CM, LANES), jnp.float32)] * 2
            + [pltpu.SemaphoreType.DMA((2,))],
            compiler_params=params(57),
            cost_estimate=cost(2),
            name="pad_edges",
        )(pads, west, east, rows)
        tops = lax.all_gather(top, "tx", axis=0, tiled=False)
        from_east = shift(west, "tx", -1, True)
        from_west = shift(east, "tx", 1, True)
        low = lax.broadcasted_iota(jnp.int32, (CP, LANES), 1) % 8 < 4
        strip = jnp.where(low, from_west[0], from_east[0])[None]
        from_south = shift(jnp.concatenate([top, strip], axis=0), "ty", 1, False)
        from_north = shift(jnp.concatenate([bottom, strip], axis=0), "ty", -1, False)
        last = interval == INTERVALS - 1
        tile_buffer = pltpu.VMEM((row_count, CP, LANES), jnp.float32)
        inner, sides, near = pl.pallas_call(
            functools.partial(inner_kernel, last),
            out_shape=(
                f32(channels, row_count, col_count) if last else f32(row_count, CM, LANES),
                f32(NSTEP, 2, 2, 2, CP, LANES),
                f32(2, H, CH, LANES),
            ),
            in_specs=[ANY, VM, VM, VM, VM, VM],
            out_specs=(ANY, VM, VM),
            scratch_shapes=[tile_buffer] * 4
            + [
                pltpu.VMEM((4, CP, LANES), jnp.float32),
                pltpu.VMEM((channels * row_count if last else 8, LANES), jnp.float32),
                pltpu.SemaphoreType.DMA((2,)),
            ],
            compiler_params=params(58),
            cost_estimate=cost(30),
            name="inner",
        )(rows, pads, from_west, from_east, mix, diff)
        wide = pltpu.VMEM((tx_count, H + 1, CP, LANES), jnp.float32)
        folds = pl.pallas_call(
            fold_kernel,
            out_shape=f32(NSTEP, 2, CP, LANES),
            in_specs=[SM, ANY, VM, VM],
            out_specs=VM,
            scratch_shapes=[
                wide,
                wide,
                pltpu.VMEM((tx_count * LANES, tx_count * LANES), jnp.bfloat16),
                pltpu.VMEM((2 * CP, tx_count * LANES), jnp.bfloat16),
                pltpu.SemaphoreType.DMA((2,)),
            ],
            compiler_params=params(58),
            cost_estimate=cost(10),
            name="fold",
        )(info, tops, mix, diff)
        side_buffer = pltpu.VMEM((2, 2 * H + 2, CP, LANES), jnp.float32)
        if last:
            done = pltpu.VMEM((2, channels * 8, LANES), jnp.float32)
        else:
            done = pltpu.VMEM((2, H, CM, LANES), jnp.float32)
        rows = pl.pallas_call(
            functools.partial(outer_kernel, last),
            out_shape=f32(*inner.shape),
            in_specs=[SM, VM, VM, VM, VM, VM, VM, VM, ANY],
            out_specs=ANY,
            scratch_shapes=[side_buffer] * 4 + [done, pltpu.SemaphoreType.DMA((2,))],
            input_output_aliases={8: 0},
            compiler_params=params(57),
            cost_estimate=cost(5),
            name="outer",
        )(info, sides, near, from_north, from_south, folds, mix, diff, inner)
    return rows.reshape(1, channels, row_count, col_count)


def solution(mesh):
    in_specs = (
        P("comp", None, "ty", "tx"),
        P("comp", None),
        P("comp", None, None),
        P("ty", "tx"),
        P("tx", "ty", None),
        P("tx", "ty"),
        P("tx", "ty"),
        P("tx"),
    )
    out_specs = P("comp", None, "ty", "tx")
    return jax.shard_map(per_device, mesh=mesh, in_specs=in_specs, out_specs=out_specs, check_vma=False)
```

```python
import functools

import jax
import jax.numpy as jnp
from jax import lax
from jax.experimental import pallas as pl
from jax.experimental.pallas import tpu as pltpu
from jax.sharding import PartitionSpec as P

NSTEP = 4
INTERVALS = 2
H = NSTEP
LANES = 128
CH = 150
CM = 152
CP = 160
MASK, FOLD, FORCE = 152, 153, 154

relaxation_speed = 0.3
flux_gain = 0.25
mix_gain = 0.1

PARAMS = pltpu.CompilerParams(vmem_limit_bytes=58 * 1024 * 1024)
VM = pl.BlockSpec(memory_space=pltpu.VMEM)
ANY = pl.BlockSpec(memory_space=pl.ANY)
SM = pl.BlockSpec(memory_space=pltpu.SMEM)


def lane_ids(rows):
    return lax.broadcasted_iota(jnp.int32, (rows, LANES), 1)


def keep_edges(units, value, unit, base, c0):
    rows = value.shape[0]
    lane = lane_ids(rows)
    near = jnp.logical_and(lane >= base, lane < base + 8)
    pltpu.store(units.at[unit, pl.ds(c0, rows)], pltpu.roll(value, (base + 4) % LANES, 1), mask=near)


def lanes_of(y):
    return (y + H) // 16 % 4, (y + H) % 16 * 8


def pack_strips(units, west_out, east_out):
    rows = west_out.shape[1]
    low = lax.rem(lane_ids(rows), 8) < 4
    for i in range(2):
        first, second = units[2 * i], units[2 * i + 1]
        west_out[i] = jnp.where(low, pltpu.roll(second, LANES - 4, 1), first)
        east_out[i] = jnp.where(low, first, pltpu.roll(second, 4, 1))


ROWS = 16


def turn_kernel(state_ref, rows_ref, west_ref, east_ref, units):
    full = CH // 8 * 8
    step = pl.program_id(0)
    flat = state_ref.reshape(CH * ROWS, LANES)
    for k in range(ROWS):
        rows_ref[k, 0:full] = flat[pl.ds(k, full, stride=ROWS), :]
        rows_ref[k, full:CH] = flat[pl.ds(full * ROWS + k, CH - full, stride=ROWS), :]
        rows_ref[k, CH:CM] = jnp.zeros((CM - CH, LANES), jnp.float32)
    for k in range(ROWS):
        keep_edges(units, rows_ref[k], lax.rem(step + (k + H) // ROWS, 4), lanes_of(k)[1], 0)

    @pl.when(step == pl.num_programs(0) - 1)
    def _():
        pack_strips(units, west_ref, east_ref)


def edge_kernel(rows_ref, west_ref, east_ref, units):
    step = pl.program_id(0)
    for k in range(ROWS):
        keep_edges(units, rows_ref[k], lax.rem(step + (k + H) // ROWS, 4), lanes_of(k)[1], 0)

    @pl.when(step == pl.num_programs(0) - 1)
    def _():
        pack_strips(units, west_ref, east_ref)


def pad_kernel(
    info_ref, take_ref, arrived_ref, fixed_ref, west_ref, east_ref, rows_hbm,
    pads_ref, west_out, east_out, bottom_ref, top_ref, units, pw_ref, pe_ref, sem,
):
    count = pads_ref.shape[0]
    copies = [
        pltpu.make_async_copy(rows_hbm.at[pl.ds(at, H)], to.at[:, pl.ds(0, CM)], sem.at[m])
        for m, (at, to) in enumerate(((0, bottom_ref), (count - H, top_ref)))
    ]
    for copy in copies:
        copy.start()
    tiles = take_ref.shape[1]
    source = jnp.where(info_ref[2] == 1, 0, tiles)
    force = jnp.zeros((count, arrived_ref.shape[2]), jnp.float32)
    for k in range(2):
        force = force + jnp.dot(
            take_ref[k].T,
            arrived_ref[pl.ds(source, tiles), k, :],
            precision=lax.Precision.HIGHEST,
            preferred_element_type=jnp.float32,
        )
    rows = (fixed_ref[0], fixed_ref[1], force[:, 0:LANES], force[:, LANES : 2 * LANES])
    for k in range(CP - CM):
        pads_ref[:, k, :] = rows[k] if k < len(rows) else jnp.zeros((count, LANES), jnp.float32)
    for y in range(count):
        keep_edges(units, pads_ref[y], *lanes_of(y), 0)
    pack_strips(units, pw_ref, pe_ref)
    west_out[:, 0:CM], west_out[:, CM:CP] = west_ref[...], pw_ref[...]
    east_out[:, 0:CM], east_out[:, CM:CP] = east_ref[...], pe_ref[...]
    for copy in copies:
        copy.wait()
    bottom_ref[:, CM:CP], top_ref[:, CM:CP] = pads_ref[0:H], pads_ref[count - H : count]


def send_kernel(info_ref, ids_ref, pick_ref, weight_ref, surface_ref, take_ref, out_ref):
    ocean = info_ref[2] == 1
    tiles, count = ids_ref.shape[0], weight_ref.shape[1]
    lane = lax.broadcasted_iota(jnp.int32, (tiles, count), 1)
    scale = jnp.where(ocean, 1.0, weight_ref[...])
    to = jnp.where(ocean, 0, tiles)
    out_ref[pl.ds(tiles - to, tiles)] = jnp.zeros((tiles, *out_ref.shape[1:]), jnp.float32)
    for k in range(2):
        asked = jnp.where(lane == ids_ref[:, k : k + 1], 1.0, 0.0)
        take = jnp.where(ocean, asked, pick_ref[k])
        take_ref[k] = take
        out_ref[pl.ds(to, tiles), k, :] = jnp.dot(
            take * scale, surface_ref[...], precision=lax.Precision.HIGHEST, preferred_element_type=jnp.float32
        )


def plan_kernel(dest_ref, target_ref, pick_ref, ids_ref):
    tiles, count = ids_ref.shape[0], dest_ref.shape[1]
    hit = lax.broadcasted_iota(jnp.int32, (tiles, count), 0) == dest_ref[...]
    before = lax.broadcasted_iota(jnp.int32, (count, count), 0) < lax.broadcasted_iota(jnp.int32, (count, count), 1)
    ones = jnp.where(hit, 1.0, 0.0)
    rank = jnp.dot(ones, jnp.where(before, 1.0, 0.0), preferred_element_type=jnp.float32)
    wanted = (target_ref[...] + 1).astype(jnp.float32)
    found = []
    for k in range(2):
        pick = jnp.where(jnp.abs(rank - k) < 0.5, ones, 0.0)
        pick_ref[k] = pick
        found.append(jnp.sum(pick * wanted, axis=1, keepdims=True) - 1.0)
    ids_ref[...] = jnp.concatenate(found, axis=1).astype(jnp.int32)


def split(x):
    high = x.astype(jnp.bfloat16)
    return high, (x - high.astype(jnp.float32)).astype(jnp.bfloat16)


def mix_pair(mix_ref, first, second):
    h0, l0 = split(first)
    h1, l1 = split(second)
    high = jnp.concatenate([h0, h1], axis=1)
    low = jnp.concatenate([l0, l1], axis=1)
    stack = jnp.concatenate([high, high, low], axis=0)
    return jnp.dot(mix_ref[...], stack, preferred_element_type=jnp.float32)


CHUNK = 40
CHUNKS = [(c, slice(c, min(c + CHUNK, CM))) for c in range(0, CM, CHUNK)]
SERVICE = slice(CM, CP)


def update_rows(spots, src, ext, mix_ref, diff_ref, put, put_ext):
    mixed = [mix_pair(mix_ref, src[spot[0]], ext[spot[0]]) for spot in spots]
    for (here, under, above), both in zip(spots, mixed):
        mask = src[here, MASK : MASK + 1, :]
        mask_ext = ext[here, MASK : MASK + 1, :]
        for c0, ch in CHUNKS:
            c, e = src[here, ch], ext[here, ch]
            lane = lane_ids(c.shape[0])
            total = pltpu.roll(jnp.where(lane == LANES - 1, e, c), 1, 1)
            total = total + pltpu.roll(jnp.where(lane == 0, e, c), LANES - 1, 1)
            total = total + (src[under, ch] + src[above, ch])
            put(here, c0, c + mask * (diff_ref[ch] * total + both[ch, 0:LANES]))
            if put_ext is None:
                continue
            total = pltpu.roll(jnp.where(lane == LANES - 1, c, e), 1, 1)
            total = total + pltpu.roll(jnp.where(lane == 0, c, e), LANES - 1, 1)
            total = total + (ext[under, ch] + ext[above, ch])
            put_ext(here, c0, e + mask_ext * (diff_ref[ch] * total + both[ch, LANES : 2 * LANES]))


def inner_kernel(
    last, rows_hbm, pads_ref, west_ref, east_ref, mix_ref, diff_ref,
    out_ref, sides_ref, near_ref, a_ref, b_ref, ea_ref, eb_ref, strip_ref, sem,
):
    count = rows_hbm.shape[0]
    copy = pltpu.make_async_copy(rows_hbm, a_ref.at[:, pl.ds(0, CM)], sem.at[0])
    copy.start()
    lane = lane_ids(CP)
    low = lax.rem(lane, 8) < 4
    for i in range(2):
        fw, fe = west_ref[i], east_ref[i]
        strip_ref[2 * i] = jnp.where(low, fw, fe)
        strip_ref[2 * i + 1] = jnp.where(low, pltpu.roll(fw, LANES - 4, 1), pltpu.roll(fe, 4, 1))

    def spread(i, _):
        for k in range(16):
            unit = lax.rem(i + (k + H) // 16, 4)
            beside = pltpu.roll(strip_ref[unit], LANES - 4 - (k + H) % 16 * 8, 1)
            ea_ref[i * 16 + k] = beside
            eb_ref[i * 16 + k, SERVICE] = beside[SERVICE]
        return 0

    lax.fori_loop(0, count // 16, spread, 0)
    copy.wait()

    def set_pads(y, _):
        a_ref[y, CM:CP] = pads_ref[y]
        b_ref[y, CM:CP] = pads_ref[y]
        return 0

    lax.fori_loop(0, count, set_pads, 0, unroll=8)
    for step in range(NSTEP):
        even = step % 2 == 0
        src, dst = (a_ref, b_ref) if even else (b_ref, a_ref)
        ext, ext_dst = (ea_ref, eb_ref) if even else (eb_ref, ea_ref)
        ends = step == NSTEP - 1
        for k in range(2):
            sides_ref[step, 0, k, 0] = src[step + k]
            sides_ref[step, 0, k, 1] = ext[step + k]
            sides_ref[step, 1, k, 0] = src[count - 1 - step - k]
            sides_ref[step, 1, k, 1] = ext[count - 1 - step - k]

        def put(y, c0, value):
            if not ends:
                dst[y, c0 : c0 + value.shape[0]] = value
            elif last:
                size = min(CHUNK, CH - c0)
                out_ref[pl.ds(c0 * count + y, size, stride=count), :] = value[0:size]
            else:
                size = min(CHUNK, CM - c0)
                out_ref[y, c0 : c0 + size] = value[0:size]

        def put_ext(y, c0, value):
            ext_dst[y, c0 : c0 + value.shape[0]] = value

        first, number = step + 1, count - 2 * step - 2

        def some(start, amount):
            spots = [(start + q, start + q - 1, start + q + 1) for q in range(amount)]
            update_rows(spots, src, ext, mix_ref, diff_ref, put, None if ends else put_ext)

        half = number // 2

        def body(i, _):
            some(first + i * half, half)
            return 0

        lax.fori_loop(0, 2, body, 0)
    if last:
        for k in range(H):
            near_ref[0, k] = out_ref[pl.ds(H + k, CH, stride=count), :]
            near_ref[1, k] = out_ref[pl.ds(count - 1 - H - k, CH, stride=count), :]


def outer_kernel(
    last, info_ref, sides_ref, near_ref, north_ref, south_ref, folds_ref, mix_ref, diff_ref, rows_hbm,
    out_hbm, a_ref, b_ref, ea_ref, eb_ref, done_ref, sem,
):
    is_fold = info_ref[0] == 1
    for k in range(H):
        a_ref[0, k] = south_ref[k]
        a_ref[1, H - 1 - k] = north_ref[k]
        ea_ref[0, k] = pltpu.roll(south_ref[H], (LANES - 4 - 8 * k) % LANES, 1)
        ea_ref[1, H - 1 - k] = pltpu.roll(north_ref[H], LANES - 4 - 8 * (H + k), 1)
        for side in range(2):
            b_ref[side, k, SERVICE] = a_ref[side, k, SERVICE]
            eb_ref[side, k, SERVICE] = ea_ref[side, k, SERVICE]
    for step in range(NSTEP):
        even = step % 2 == 0
        src, dst = (a_ref, b_ref) if even else (b_ref, a_ref)
        ext, ext_dst = (ea_ref, eb_ref) if even else (eb_ref, ea_ref)
        for side in range(2):
            for k in range(2):
                src[side, H + step + k] = sides_ref[step, side, k, 0]
                ext[side, H + step + k] = sides_ref[step, side, k, 1]
            dst[side, H + step, SERVICE] = sides_ref[step, side, 0, 0, SERVICE]
            ext_dst[side, H + step, SERVICE] = sides_ref[step, side, 0, 1, SERVICE]

        @pl.when(is_fold)
        def _():
            src[1, H - 1] = folds_ref[step, 0]
            ext[1, H - 1] = folds_ref[step, 1]

        ends = step == NSTEP - 1

        def put(spot, c0, value):
            side, k = spot
            if not ends:
                dst[side, k, c0 : c0 + value.shape[0]] = value
            elif last:
                y = k - H if side == 0 else 7 - (k - H)
                size = min(CHUNK, CH - c0)
                done_ref[side, pl.ds(c0 * 8 + y, size, stride=8), :] = value[0:size]
            else:
                y = k - H if side == 0 else H - 1 - (k - H)
                size = min(CHUNK, CM - c0)
                done_ref[side, y, c0 : c0 + size] = value[0:size]

        def put_ext(spot, c0, value):
            side, k = spot
            ext_dst[side, k, c0 : c0 + value.shape[0]] = value

        spots = [((m, k), (m, k - 1), (m, k + 1)) for m in range(2) for k in range(step + 1, step + 1 + H)]
        update_rows(spots, At(src), At(ext), mix_ref, diff_ref, put, None if ends else put_ext)
    if last:
        count = out_hbm.shape[1]
        for k in range(H):
            done_ref[0, pl.ds(H + k, CH, stride=8), :] = near_ref[0, k]
            done_ref[1, pl.ds(H - 1 - k, CH, stride=8), :] = near_ref[1, k]
        copies = [
            pltpu.make_async_copy(done_ref.at[m].reshape(CH, 8, LANES), out_hbm.at[:, pl.ds(at, 8)], sem.at[m])
            for m, at in ((0, 0), (1, count - 8))
        ]
    else:
        count = out_hbm.shape[0]
        copies = [
            pltpu.make_async_copy(done_ref.at[m], out_hbm.at[pl.ds(at, H)], sem.at[m]) for m, at in ((0, 0), (1, count - H))
        ]
    for copy in copies:
        copy.start()
    for copy in copies:
        copy.wait()


class At:
    def __init__(self, ref):
        self.ref = ref

    def __getitem__(self, key):
        if isinstance(key[0], tuple):
            return self.ref[(*key[0], *key[1:])]
        return self.ref[key]


def fold_kernel(info_ref, top_hbm, mix_ref, diff_ref, out_ref, wa_ref, wb_ref, fold_ref, lhs_ref, sem):
    tiles = wa_ref.shape[0]
    own = info_ref[1]

    @pl.when(info_ref[0] == 1)
    def _():
        tops = pltpu.make_async_copy(top_hbm, wa_ref.at[:, pl.ds(0, H)], sem.at[0])
        service = pltpu.make_async_copy(
            top_hbm.at[:, :, pl.ds(CM, CP - CM)], wb_ref.at[:, pl.ds(0, H), pl.ds(CM, CP - CM)], sem.at[1]
        )
        tops.start()
        service.start()
        tops.wait()
        service.wait()
        for j in range(tiles):
            source = wa_ref[j, H - 1, FOLD : FOLD + 1, :]
            for block in range(tiles):
                at = (lax.broadcasted_iota(jnp.int32, (LANES, LANES), 0) + block * LANES).astype(jnp.float32)
                hit = jnp.where(at == source, 1.0, 0.0).astype(jnp.bfloat16)
                fold_ref[block * LANES : (block + 1) * LANES, j * LANES : (j + 1) * LANES] = hit
        lane = lane_ids(CP)
        for step in range(NSTEP):
            w_src, w_dst = (wa_ref, wb_ref) if step % 2 == 0 else (wb_ref, wa_ref)
            for j in range(tiles):
                high, below = split(w_src[j, H - 1])
                lhs_ref[0:CP, j * LANES : (j + 1) * LANES] = high
                lhs_ref[CP : 2 * CP, j * LANES : (j + 1) * LANES] = below
            for p in range(tiles // 2):
                both = jnp.dot(
                    lhs_ref[...], fold_ref[:, 2 * p * LANES : 2 * (p + 1) * LANES], preferred_element_type=jnp.float32
                )
                both = both[0:CP] + both[CP : 2 * CP]
                w_src[2 * p, H] = both[:, 0:LANES]
                w_src[2 * p + 1, H] = both[:, LANES : 2 * LANES]
            out_ref[step, 0] = w_src[own, H]
            before, after = w_src[lax.rem(own + tiles - 1, tiles), H], w_src[lax.rem(own + 1, tiles), H]
            out_ref[step, 1] = jnp.where(lane < LANES // 2, after, before)
            if step == NSTEP - 1:
                continue

            for k in range(step + 1, H):
                mixed = [mix_pair(mix_ref, w_src[j, k], w_src[j + 1, k]) for j in range(0, tiles, 2)]
                for here in range(tiles):
                    mask = w_src[here, k, MASK : MASK + 1, :]
                    left, right = (here + tiles - 1) % tiles, (here + 1) % tiles
                    m = here % 2
                    for _, ch in CHUNKS:
                        c = w_src[here, k, ch]
                        part_lane = lane_ids(c.shape[0])
                        total = pltpu.roll(jnp.where(part_lane == LANES - 1, w_src[left, k, ch], c), 1, 1)
                        total = total + pltpu.roll(jnp.where(part_lane == 0, w_src[right, k, ch], c), LANES - 1, 1)
                        total = total + (w_src[here, k - 1, ch] + w_src[here, k + 1, ch])
                        change = diff_ref[ch] * total + mixed[here // 2][ch, m * LANES : (m + 1) * LANES]
                        w_dst[here, k, ch] = c + mask * change


def cost(us):
    return pl.CostEstimate(flops=int(us * 1e9), bytes_accessed=int(us * 3e6), transcendentals=0)


def f32(*shape):
    return jax.ShapeDtypeStruct(shape, jnp.float32)


def shift(x, axis, by, closed):
    count = lax.axis_size(axis)
    pairs = [(i, (i + by) % count) for i in range(count) if closed or 0 <= i + by < count]
    return lax.ppermute(x, axis, pairs)


def per_device(state, diffusivity, mixing, ocean_mask, flux_dest, flux_target, flux_weight, fold_source):
    _, channels, row_count, col_count = state.shape
    levels = channels // 2
    tx_count = lax.axis_size("tx")
    is_ocean = lax.axis_index("comp") == 1
    northmost = lax.axis_index("ty") == lax.axis_size("ty") - 1
    tile_count = lax.axis_size("ty") * tx_count
    slots = max(2, 2 * row_count // tile_count)
    info = jnp.stack([jnp.logical_and(is_ocean, northmost).astype(jnp.int32), lax.axis_index("tx").astype(jnp.int32), is_ocean.astype(jnp.int32)])

    diffuse = diffusivity[0]
    service = jnp.where(is_ocean, flux_gain, relaxation_speed)
    own_surface = jnp.where(is_ocean, 0.0, relaxation_speed)
    ids = jnp.arange(channels)
    surface_row = jnp.logical_or(ids == 0, ids == levels)
    centre = 4.0 * diffuse + jnp.where(surface_row, own_surface, 0.0)
    matrix = mix_gain * mixing[0] - jnp.where(ids[:, None] == ids[None, :], centre[:, None], 0.0)
    matrix = jnp.pad(matrix, ((0, CP - channels), (0, CP - channels)))
    at_row = lax.broadcasted_iota(jnp.int32, (CP, CP), 0)
    at_col = lax.broadcasted_iota(jnp.int32, (CP, CP), 1)
    forced = jnp.logical_or(
        jnp.logical_and(at_row == 0, at_col == FORCE), jnp.logical_and(at_row == levels, at_col == FORCE + 1)
    )
    matrix = jnp.where(forced, service, matrix)
    high = lax.reduce_precision(matrix, 8, 7)
    rest = (matrix - high).astype(jnp.bfloat16)
    high = high.astype(jnp.bfloat16)
    mix = jnp.concatenate([high, rest, high], axis=1)[:CM]
    diff = jnp.broadcast_to(jnp.pad(diffuse, (0, CM - channels))[:, None], (CM, LANES))

    pick, out_ids = pl.pallas_call(
        plan_kernel,
        out_shape=(f32(slots, tile_count, row_count), jax.ShapeDtypeStruct((tile_count, slots), jnp.int32)),
        in_specs=[VM, VM],
        out_specs=(VM, VM),
        compiler_params=PARAMS,
        name="plan",
    )(flux_dest[:, :, 0], flux_target)
    in_ids = lax.all_to_all(out_ids, ("ty", "tx"), split_axis=0, concat_axis=0, tiled=True)
    everyone = ("comp", "ty", "tx")

    sea_mask = jnp.where(is_ocean, ocean_mask.astype(jnp.float32), 1.0)
    fold_rows = jnp.broadcast_to(fold_source.astype(jnp.float32)[None, :], sea_mask.shape)
    fixed = jnp.stack([sea_mask, fold_rows])

    rows = None
    for interval in range(INTERVALS):
        if interval == 0:
            surface = jnp.concatenate([state[0, 0], state[0, levels]], axis=1)
            rows, west, east = pl.pallas_call(
                turn_kernel,
                grid=(row_count // ROWS,),
                out_shape=(f32(row_count, CM, LANES), f32(2, CM, LANES), f32(2, CM, LANES)),
                in_specs=[pl.BlockSpec((CH, ROWS, LANES), lambda i: (0, i, 0))],
                out_specs=(
                    pl.BlockSpec((ROWS, CM, LANES), lambda i: (i, 0, 0)),
                    pl.BlockSpec((2, CM, LANES), lambda i: (0, 0, 0)),
                    pl.BlockSpec((2, CM, LANES), lambda i: (0, 0, 0)),
                ),
                scratch_shapes=[pltpu.VMEM((4, CM, LANES), jnp.float32)],
                compiler_params=PARAMS,
                cost_estimate=cost(10),
                name="turn",
            )(state[0])
        else:
            surface = lax.optimization_barrier(jnp.concatenate([rows[:, 0], rows[:, levels]], axis=1))
            west, east = pl.pallas_call(
                edge_kernel,
                grid=(row_count // ROWS,),
                out_shape=(f32(2, CM, LANES), f32(2, CM, LANES)),
                in_specs=[pl.BlockSpec((ROWS, CM, LANES), lambda i: (i, 0, 0))],
                out_specs=(
                    pl.BlockSpec((2, CM, LANES), lambda i: (0, 0, 0)),
                    pl.BlockSpec((2, CM, LANES), lambda i: (0, 0, 0)),
                ),
                scratch_shapes=[pltpu.VMEM((4, CM, LANES), jnp.float32)],
                compiler_params=PARAMS,
                cost_estimate=cost(5),
                name="edges",
            )(rows)
        take, outgoing = pl.pallas_call(
            send_kernel,
            out_shape=(f32(slots, tile_count, row_count), f32(2 * tile_count, slots, 2 * col_count)),
            in_specs=[SM, VM, VM, VM, VM],
            out_specs=(VM, VM),
            compiler_params=PARAMS,
            cost_estimate=cost(1),
            name="send",
        )(info, in_ids, pick, flux_weight, surface)
        arrived = lax.all_to_all(outgoing, everyone, split_axis=0, concat_axis=0, tiled=True)
        arrived, west, east, diff = lax.optimization_barrier((arrived, west, east, diff))
        pads, west, east, bottom, top = pl.pallas_call(
            pad_kernel,
            out_shape=(f32(row_count, CP - CM, LANES), f32(2, CP, LANES), f32(2, CP, LANES), f32(H, CP, LANES), f32(H, CP, LANES)),
            in_specs=[SM, VM, VM, VM, VM, VM, ANY],
            out_specs=(VM, VM, VM, VM, VM),
            scratch_shapes=[pltpu.VMEM((4, CP - CM, LANES), jnp.float32)]
            + [pltpu.VMEM((2, CP - CM, LANES), jnp.float32)] * 2
            + [pltpu.SemaphoreType.DMA((2,))],
            compiler_params=PARAMS,
            cost_estimate=cost(2),
            name="pad_edges",
        )(info, take, arrived, fixed, west, east, rows)
        tops = lax.all_gather(top, "tx", axis=0, tiled=False)
        from_east = shift(west, "tx", -1, True)
        from_west = shift(east, "tx", 1, True)
        low = lax.broadcasted_iota(jnp.int32, (CP, LANES), 1) % 8 < 4
        strip = jnp.where(low, from_west[0], from_east[0])[None]
        from_south = shift(jnp.concatenate([top, strip], axis=0), "ty", 1, False)
        from_north = shift(jnp.concatenate([bottom, strip], axis=0), "ty", -1, False)
        last = interval == INTERVALS - 1
        tile_buffer = pltpu.VMEM((row_count, CP, LANES), jnp.float32)
        inner, sides, near = pl.pallas_call(
            functools.partial(inner_kernel, last),
            out_shape=(
                f32(channels * row_count, col_count) if last else f32(row_count, CM, LANES),
                f32(NSTEP, 2, 2, 2, CP, LANES),
                f32(2, H, CH, LANES),
            ),
            in_specs=[ANY, VM, VM, VM, VM, VM],
            out_specs=(VM, VM, VM),
            scratch_shapes=[tile_buffer] * 4 + [pltpu.VMEM((4, CP, LANES), jnp.float32), pltpu.SemaphoreType.DMA((1,))],
            compiler_params=PARAMS,
            cost_estimate=cost(30),
            name="inner",
        )(rows, pads, from_west, from_east, mix, diff)
        wide = pltpu.VMEM((tx_count, H + 1, CP, LANES), jnp.float32)
        folds = pl.pallas_call(
            fold_kernel,
            out_shape=f32(NSTEP, 2, CP, LANES),
            in_specs=[SM, ANY, VM, VM],
            out_specs=VM,
            scratch_shapes=[
                wide,
                wide,
                pltpu.VMEM((tx_count * LANES, tx_count * LANES), jnp.bfloat16),
                pltpu.VMEM((2 * CP, tx_count * LANES), jnp.bfloat16),
                pltpu.SemaphoreType.DMA((2,)),
            ],
            compiler_params=PARAMS,
            cost_estimate=cost(10),
            name="fold",
        )(info, tops, mix, diff)
        side_buffer = pltpu.VMEM((2, 2 * H + 2, CP, LANES), jnp.float32)
        if last:
            inner = inner.reshape(channels, row_count, col_count)
            done = pltpu.VMEM((2, channels * 8, LANES), jnp.float32)
        else:
            done = pltpu.VMEM((2, H, CM, LANES), jnp.float32)
        rows = pl.pallas_call(
            functools.partial(outer_kernel, last),
            out_shape=f32(*inner.shape),
            in_specs=[SM, VM, VM, VM, VM, VM, VM, VM, ANY],
            out_specs=ANY,
            scratch_shapes=[side_buffer] * 4 + [done, pltpu.SemaphoreType.DMA((2,))],
            input_output_aliases={8: 0},
            compiler_params=PARAMS,
            cost_estimate=cost(5),
            name="outer",
        )(info, sides, near, from_north, from_south, folds, mix, diff, inner)
    return rows.reshape(1, channels, row_count, col_count)


def solution(mesh):
    in_specs = (
        P("comp", None, "ty", "tx"),
        P("comp", None),
        P("comp", None, None),
        P("ty", "tx"),
        P("tx", "ty", None),
        P("tx", "ty"),
        P("tx", "ty"),
        P("tx"),
    )
    out_specs = P("comp", None, "ty", "tx")
    return jax.shard_map(per_device, mesh=mesh, in_specs=in_specs, out_specs=out_specs, check_vma=False)
```

```python
import functools

import jax
import jax.numpy as jnp
from jax import lax
from jax.experimental import pallas as pl
from jax.experimental.pallas import tpu as pltpu
from jax.sharding import PartitionSpec as P

NSTEP = 4
INTERVALS = 2
H = NSTEP
LANES = 128
CH = 150
CM = 152
CP = 160
MASK, FOLD, FORCE = 152, 153, 154

relaxation_speed = 0.3
flux_gain = 0.25
mix_gain = 0.1

PARAMS = pltpu.CompilerParams(vmem_limit_bytes=58 * 1024 * 1024)
VM = pl.BlockSpec(memory_space=pltpu.VMEM)
ANY = pl.BlockSpec(memory_space=pl.ANY)
SM = pl.BlockSpec(memory_space=pltpu.SMEM)


def lane_ids(rows):
    return lax.broadcasted_iota(jnp.int32, (rows, LANES), 1)


def keep_edges(units, value, unit, base, c0):
    rows = value.shape[0]
    lane = lane_ids(rows)
    near = jnp.logical_and(lane >= base, lane < base + 8)
    pltpu.store(units.at[unit, pl.ds(c0, rows)], pltpu.roll(value, (base + 4) % LANES, 1), mask=near)


def lanes_of(y):
    return (y + H) // 16 % 4, (y + H) % 16 * 8


def pack_strips(units, west_out, east_out):
    rows = west_out.shape[1]
    low = lax.rem(lane_ids(rows), 8) < 4
    for i in range(2):
        first, second = units[2 * i], units[2 * i + 1]
        west_out[i] = jnp.where(low, pltpu.roll(second, LANES - 4, 1), first)
        east_out[i] = jnp.where(low, first, pltpu.roll(second, 4, 1))


ROWS = 16


def turn_kernel(state_ref, rows_ref, west_ref, east_ref, units):
    full = CH // 8 * 8
    step = pl.program_id(0)
    flat = state_ref.reshape(CH * ROWS, LANES)
    for k in range(ROWS):
        rows_ref[k, 0:full] = flat[pl.ds(k, full, stride=ROWS), :]
        rows_ref[k, full:CH] = flat[pl.ds(full * ROWS + k, CH - full, stride=ROWS), :]
        rows_ref[k, CH:CM] = jnp.zeros((CM - CH, LANES), jnp.float32)
    for k in range(ROWS):
        keep_edges(units, rows_ref[k], lax.rem(step + (k + H) // ROWS, 4), lanes_of(k)[1], 0)

    @pl.when(step == pl.num_programs(0) - 1)
    def _():
        pack_strips(units, west_ref, east_ref)


def edge_kernel(rows_ref, west_ref, east_ref, units):
    step = pl.program_id(0)
    for k in range(ROWS):
        keep_edges(units, rows_ref[k], lax.rem(step + (k + H) // ROWS, 4), lanes_of(k)[1], 0)

    @pl.when(step == pl.num_programs(0) - 1)
    def _():
        pack_strips(units, west_ref, east_ref)


def pad_kernel(pads_ref, west_ref, east_ref, rows_hbm, west_out, east_out, bottom_ref, top_ref, units, pw_ref, pe_ref, sem):
    count = pads_ref.shape[0]
    copies = [
        pltpu.make_async_copy(rows_hbm.at[pl.ds(at, H)], to.at[:, pl.ds(0, CM)], sem.at[m])
        for m, (at, to) in enumerate(((0, bottom_ref), (count - H, top_ref)))
    ]
    for copy in copies:
        copy.start()
    for y in range(count):
        keep_edges(units, pads_ref[y], *lanes_of(y), 0)
    pack_strips(units, pw_ref, pe_ref)
    west_out[:, 0:CM], west_out[:, CM:CP] = west_ref[...], pw_ref[...]
    east_out[:, 0:CM], east_out[:, CM:CP] = east_ref[...], pe_ref[...]
    for copy in copies:
        copy.wait()
    bottom_ref[:, CM:CP], top_ref[:, CM:CP] = pads_ref[0:H], pads_ref[count - H : count]


def plan_kernel(dest_ref, target_ref, pick_ref, ids_ref):
    tiles, count = ids_ref.shape[0], dest_ref.shape[1]
    hit = lax.broadcasted_iota(jnp.int32, (tiles, count), 0) == dest_ref[...]
    before = lax.broadcasted_iota(jnp.int32, (count, count), 0) < lax.broadcasted_iota(jnp.int32, (count, count), 1)
    ones = jnp.where(hit, 1.0, 0.0)
    rank = jnp.dot(ones, jnp.where(before, 1.0, 0.0), preferred_element_type=jnp.float32)
    wanted = (target_ref[...] + 1).astype(jnp.float32)
    found = []
    for k in range(2):
        pick = jnp.where(jnp.abs(rank - k) < 0.5, ones, 0.0)
        pick_ref[pl.ds(k, tiles, stride=2), :] = pick
        found.append(jnp.sum(pick * wanted, axis=1, keepdims=True) - 1.0)
    ids_ref[...] = jnp.concatenate(found, axis=1).astype(jnp.int32)


def split(x):
    high = x.astype(jnp.bfloat16)
    return high, (x - high.astype(jnp.float32)).astype(jnp.bfloat16)


def mix_pair(mix_ref, first, second):
    h0, l0 = split(first)
    h1, l1 = split(second)
    high = jnp.concatenate([h0, h1], axis=1)
    low = jnp.concatenate([l0, l1], axis=1)
    stack = jnp.concatenate([high, high, low], axis=0)
    return jnp.dot(mix_ref[...], stack, preferred_element_type=jnp.float32)


CHUNK = 40
CHUNKS = [(c, slice(c, min(c + CHUNK, CM))) for c in range(0, CM, CHUNK)]
SERVICE = slice(CM, CP)


def update_rows(spots, src, ext, mix_ref, diff_ref, put, put_ext):
    mixed = [mix_pair(mix_ref, src[spot[0]], ext[spot[0]]) for spot in spots]
    for (here, under, above), both in zip(spots, mixed):
        mask = src[here, MASK : MASK + 1, :]
        mask_ext = ext[here, MASK : MASK + 1, :]
        for c0, ch in CHUNKS:
            c, e = src[here, ch], ext[here, ch]
            lane = lane_ids(c.shape[0])
            total = pltpu.roll(jnp.where(lane == LANES - 1, e, c), 1, 1)
            total = total + pltpu.roll(jnp.where(lane == 0, e, c), LANES - 1, 1)
            total = total + (src[under, ch] + src[above, ch])
            put(here, c0, c + mask * (diff_ref[ch] * total + both[ch, 0:LANES]))
            if put_ext is None:
                continue
            total = pltpu.roll(jnp.where(lane == LANES - 1, c, e), 1, 1)
            total = total + pltpu.roll(jnp.where(lane == 0, c, e), LANES - 1, 1)
            total = total + (ext[under, ch] + ext[above, ch])
            put_ext(here, c0, e + mask_ext * (diff_ref[ch] * total + both[ch, LANES : 2 * LANES]))


def inner_kernel(
    last, rows_hbm, pads_ref, west_ref, east_ref, mix_ref, diff_ref,
    out_ref, sides_ref, near_ref, a_ref, b_ref, ea_ref, eb_ref, strip_ref, sem,
):
    count = rows_hbm.shape[0]
    copy = pltpu.make_async_copy(rows_hbm, a_ref.at[:, pl.ds(0, CM)], sem.at[0])
    copy.start()
    lane = lane_ids(CP)
    low = lax.rem(lane, 8) < 4
    for i in range(2):
        fw, fe = west_ref[i], east_ref[i]
        strip_ref[2 * i] = jnp.where(low, fw, fe)
        strip_ref[2 * i + 1] = jnp.where(low, pltpu.roll(fw, LANES - 4, 1), pltpu.roll(fe, 4, 1))

    def spread(i, _):
        for k in range(16):
            unit = lax.rem(i + (k + H) // 16, 4)
            beside = pltpu.roll(strip_ref[unit], LANES - 4 - (k + H) % 16 * 8, 1)
            ea_ref[i * 16 + k] = beside
            eb_ref[i * 16 + k, SERVICE] = beside[SERVICE]
        return 0

    lax.fori_loop(0, count // 16, spread, 0)
    copy.wait()

    def set_pads(y, _):
        a_ref[y, CM:CP] = pads_ref[y]
        b_ref[y, CM:CP] = pads_ref[y]
        return 0

    lax.fori_loop(0, count, set_pads, 0, unroll=8)
    for step in range(NSTEP):
        even = step % 2 == 0
        src, dst = (a_ref, b_ref) if even else (b_ref, a_ref)
        ext, ext_dst = (ea_ref, eb_ref) if even else (eb_ref, ea_ref)
        ends = step == NSTEP - 1
        for k in range(2):
            sides_ref[step, 0, k, 0] = src[step + k]
            sides_ref[step, 0, k, 1] = ext[step + k]
            sides_ref[step, 1, k, 0] = src[count - 1 - step - k]
            sides_ref[step, 1, k, 1] = ext[count - 1 - step - k]

        def put(y, c0, value):
            if not ends:
                dst[y, c0 : c0 + value.shape[0]] = value
            elif last:
                size = min(CHUNK, CH - c0)
                out_ref[pl.ds(c0 * count + y, size, stride=count), :] = value[0:size]
            else:
                size = min(CHUNK, CM - c0)
                out_ref[y, c0 : c0 + size] = value[0:size]

        def put_ext(y, c0, value):
            ext_dst[y, c0 : c0 + value.shape[0]] = value

        first, number = step + 1, count - 2 * step - 2

        def some(start, amount):
            spots = [(start + q, start + q - 1, start + q + 1) for q in range(amount)]
            update_rows(spots, src, ext, mix_ref, diff_ref, put, None if ends else put_ext)

        half = number // 2

        def body(i, _):
            some(first + i * half, half)
            return 0

        lax.fori_loop(0, 2, body, 0)
    if last:
        for k in range(H):
            near_ref[0, k] = out_ref[pl.ds(H + k, CH, stride=count), :]
            near_ref[1, k] = out_ref[pl.ds(count - 1 - H - k, CH, stride=count), :]


def outer_kernel(
    last, info_ref, sides_ref, near_ref, north_ref, south_ref, folds_ref, mix_ref, diff_ref, rows_hbm,
    out_hbm, a_ref, b_ref, ea_ref, eb_ref, done_ref, sem,
):
    is_fold = info_ref[0] == 1
    for k in range(H):
        a_ref[0, k] = south_ref[k]
        a_ref[1, H - 1 - k] = north_ref[k]
        ea_ref[0, k] = pltpu.roll(south_ref[H], (LANES - 4 - 8 * k) % LANES, 1)
        ea_ref[1, H - 1 - k] = pltpu.roll(north_ref[H], LANES - 4 - 8 * (H + k), 1)
        for side in range(2):
            b_ref[side, k, SERVICE] = a_ref[side, k, SERVICE]
            eb_ref[side, k, SERVICE] = ea_ref[side, k, SERVICE]
    for step in range(NSTEP):
        even = step % 2 == 0
        src, dst = (a_ref, b_ref) if even else (b_ref, a_ref)
        ext, ext_dst = (ea_ref, eb_ref) if even else (eb_ref, ea_ref)
        for side in range(2):
            for k in range(2):
                src[side, H + step + k] = sides_ref[step, side, k, 0]
                ext[side, H + step + k] = sides_ref[step, side, k, 1]
            dst[side, H + step, SERVICE] = sides_ref[step, side, 0, 0, SERVICE]
            ext_dst[side, H + step, SERVICE] = sides_ref[step, side, 0, 1, SERVICE]

        @pl.when(is_fold)
        def _():
            src[1, H - 1] = folds_ref[step, 0]
            ext[1, H - 1] = folds_ref[step, 1]

        ends = step == NSTEP - 1

        def put(spot, c0, value):
            side, k = spot
            if not ends:
                dst[side, k, c0 : c0 + value.shape[0]] = value
            elif last:
                y = k - H if side == 0 else 7 - (k - H)
                size = min(CHUNK, CH - c0)
                done_ref[side, pl.ds(c0 * 8 + y, size, stride=8), :] = value[0:size]
            else:
                y = k - H if side == 0 else H - 1 - (k - H)
                size = min(CHUNK, CM - c0)
                done_ref[side, y, c0 : c0 + size] = value[0:size]

        def put_ext(spot, c0, value):
            side, k = spot
            ext_dst[side, k, c0 : c0 + value.shape[0]] = value

        spots = [((m, k), (m, k - 1), (m, k + 1)) for m in range(2) for k in range(step + 1, step + 1 + H)]
        update_rows(spots, At(src), At(ext), mix_ref, diff_ref, put, None if ends else put_ext)
    if last:
        count = out_hbm.shape[1]
        for k in range(H):
            done_ref[0, pl.ds(H + k, CH, stride=8), :] = near_ref[0, k]
            done_ref[1, pl.ds(H - 1 - k, CH, stride=8), :] = near_ref[1, k]
        copies = [
            pltpu.make_async_copy(done_ref.at[m].reshape(CH, 8, LANES), out_hbm.at[:, pl.ds(at, 8)], sem.at[m])
            for m, at in ((0, 0), (1, count - 8))
        ]
    else:
        count = out_hbm.shape[0]
        copies = [
            pltpu.make_async_copy(done_ref.at[m], out_hbm.at[pl.ds(at, H)], sem.at[m]) for m, at in ((0, 0), (1, count - H))
        ]
    for copy in copies:
        copy.start()
    for copy in copies:
        copy.wait()


class At:
    def __init__(self, ref):
        self.ref = ref

    def __getitem__(self, key):
        if isinstance(key[0], tuple):
            return self.ref[(*key[0], *key[1:])]
        return self.ref[key]


def fold_kernel(info_ref, top_hbm, mix_ref, diff_ref, out_ref, wa_ref, wb_ref, fold_ref, lhs_ref, sem):
    tiles = wa_ref.shape[0]
    own = info_ref[1]

    @pl.when(info_ref[0] == 1)
    def _():
        tops = pltpu.make_async_copy(top_hbm, wa_ref.at[:, pl.ds(0, H)], sem.at[0])
        service = pltpu.make_async_copy(
            top_hbm.at[:, :, pl.ds(CM, CP - CM)], wb_ref.at[:, pl.ds(0, H), pl.ds(CM, CP - CM)], sem.at[1]
        )
        tops.start()
        service.start()
        tops.wait()
        service.wait()
        for j in range(tiles):
            source = wa_ref[j, H - 1, FOLD : FOLD + 1, :]
            for block in range(tiles):
                at = (lax.broadcasted_iota(jnp.int32, (LANES, LANES), 0) + block * LANES).astype(jnp.float32)
                hit = jnp.where(at == source, 1.0, 0.0).astype(jnp.bfloat16)
                fold_ref[block * LANES : (block + 1) * LANES, j * LANES : (j + 1) * LANES] = hit
        lane = lane_ids(CP)
        for step in range(NSTEP):
            w_src, w_dst = (wa_ref, wb_ref) if step % 2 == 0 else (wb_ref, wa_ref)
            for j in range(tiles):
                high, below = split(w_src[j, H - 1])
                lhs_ref[0:CP, j * LANES : (j + 1) * LANES] = high
                lhs_ref[CP : 2 * CP, j * LANES : (j + 1) * LANES] = below
            for p in range(tiles // 2):
                both = jnp.dot(
                    lhs_ref[...], fold_ref[:, 2 * p * LANES : 2 * (p + 1) * LANES], preferred_element_type=jnp.float32
                )
                both = both[0:CP] + both[CP : 2 * CP]
                w_src[2 * p, H] = both[:, 0:LANES]
                w_src[2 * p + 1, H] = both[:, LANES : 2 * LANES]
            out_ref[step, 0] = w_src[own, H]
            before, after = w_src[lax.rem(own + tiles - 1, tiles), H], w_src[lax.rem(own + 1, tiles), H]
            out_ref[step, 1] = jnp.where(lane < LANES // 2, after, before)
            if step == NSTEP - 1:
                continue

            for k in range(step + 1, H):
                mixed = [mix_pair(mix_ref, w_src[j, k], w_src[j + 1, k]) for j in range(0, tiles, 2)]
                for here in range(tiles):
                    mask = w_src[here, k, MASK : MASK + 1, :]
                    left, right = (here + tiles - 1) % tiles, (here + 1) % tiles
                    m = here % 2
                    for _, ch in CHUNKS:
                        c = w_src[here, k, ch]
                        part_lane = lane_ids(c.shape[0])
                        total = pltpu.roll(jnp.where(part_lane == LANES - 1, w_src[left, k, ch], c), 1, 1)
                        total = total + pltpu.roll(jnp.where(part_lane == 0, w_src[right, k, ch], c), LANES - 1, 1)
                        total = total + (w_src[here, k - 1, ch] + w_src[here, k + 1, ch])
                        change = diff_ref[ch] * total + mixed[here // 2][ch, m * LANES : (m + 1) * LANES]
                        w_dst[here, k, ch] = c + mask * change


def cost(us):
    return pl.CostEstimate(flops=int(us * 1e9), bytes_accessed=int(us * 3e6), transcendentals=0)


def f32(*shape):
    return jax.ShapeDtypeStruct(shape, jnp.float32)


def shift(x, axis, by, closed):
    count = lax.axis_size(axis)
    pairs = [(i, (i + by) % count) for i in range(count) if closed or 0 <= i + by < count]
    return lax.ppermute(x, axis, pairs)


def per_device(state, diffusivity, mixing, ocean_mask, flux_dest, flux_target, flux_weight, fold_source):
    _, channels, row_count, col_count = state.shape
    levels = channels // 2
    tx_count = lax.axis_size("tx")
    is_ocean = lax.axis_index("comp") == 1
    northmost = lax.axis_index("ty") == lax.axis_size("ty") - 1
    tile_count = lax.axis_size("ty") * tx_count
    slots = max(2, 2 * row_count // tile_count)
    info = jnp.stack([jnp.logical_and(is_ocean, northmost).astype(jnp.int32), lax.axis_index("tx").astype(jnp.int32)])

    diffuse = diffusivity[0]
    service = jnp.where(is_ocean, flux_gain, relaxation_speed)
    own_surface = jnp.where(is_ocean, 0.0, relaxation_speed)
    ids = jnp.arange(channels)
    surface_row = jnp.logical_or(ids == 0, ids == levels)
    centre = 4.0 * diffuse + jnp.where(surface_row, own_surface, 0.0)
    matrix = mix_gain * mixing[0] - jnp.where(ids[:, None] == ids[None, :], centre[:, None], 0.0)
    matrix = jnp.pad(matrix, ((0, CP - channels), (0, CP - channels)))
    at_row = lax.broadcasted_iota(jnp.int32, (CP, CP), 0)
    at_col = lax.broadcasted_iota(jnp.int32, (CP, CP), 1)
    forced = jnp.logical_or(
        jnp.logical_and(at_row == 0, at_col == FORCE), jnp.logical_and(at_row == levels, at_col == FORCE + 1)
    )
    matrix = jnp.where(forced, service, matrix)
    high = lax.reduce_precision(matrix, 8, 7)
    rest = (matrix - high).astype(jnp.bfloat16)
    high = high.astype(jnp.bfloat16)
    mix = jnp.concatenate([high, rest, high], axis=1)[:CM]
    diff = jnp.broadcast_to(jnp.pad(diffuse, (0, CM - channels))[:, None], (CM, LANES))

    pick, out_ids = pl.pallas_call(
        plan_kernel,
        out_shape=(f32(tile_count * slots, row_count), jax.ShapeDtypeStruct((tile_count, slots), jnp.int32)),
        in_specs=[VM, VM],
        out_specs=(VM, VM),
        compiler_params=PARAMS,
        name="plan",
    )(flux_dest[:, :, 0], flux_target)
    in_ids = lax.all_to_all(out_ids, ("ty", "tx"), split_axis=0, concat_axis=0, tiled=True)
    place = (in_ids.reshape(-1)[None, :] == jnp.arange(row_count, dtype=jnp.int32)[:, None]).astype(jnp.float32)
    here = jnp.where(is_ocean, 1.0, 0.0)
    send_mat = jnp.where(is_ocean, place.T, pick * flux_weight[0][None, :])
    send_mat = jnp.concatenate([send_mat * here, send_mat * (1.0 - here)], axis=0)
    take_mat = jnp.where(is_ocean, place, pick.T)
    take_mat = jnp.concatenate([take_mat * here, take_mat * (1.0 - here)], axis=1)
    everyone = ("comp", "ty", "tx")

    sea_mask = jnp.where(is_ocean, ocean_mask.astype(jnp.float32), 1.0)
    fold_rows = jnp.broadcast_to(fold_source.astype(jnp.float32)[None, :], sea_mask.shape)
    blank = jnp.zeros_like(sea_mask)
    best = lax.Precision.HIGHEST

    rows = None
    for interval in range(INTERVALS):
        if interval == 0:
            surface = jnp.concatenate([state[0, 0], state[0, levels]], axis=1)
            rows, west, east = pl.pallas_call(
                turn_kernel,
                grid=(row_count // ROWS,),
                out_shape=(f32(row_count, CM, LANES), f32(2, CM, LANES), f32(2, CM, LANES)),
                in_specs=[pl.BlockSpec((CH, ROWS, LANES), lambda i: (0, i, 0))],
                out_specs=(
                    pl.BlockSpec((ROWS, CM, LANES), lambda i: (i, 0, 0)),
                    pl.BlockSpec((2, CM, LANES), lambda i: (0, 0, 0)),
                    pl.BlockSpec((2, CM, LANES), lambda i: (0, 0, 0)),
                ),
                scratch_shapes=[pltpu.VMEM((4, CM, LANES), jnp.float32)],
                compiler_params=PARAMS,
                cost_estimate=cost(10),
                name="turn",
            )(state[0])
        else:
            surface = lax.optimization_barrier(jnp.concatenate([rows[:, 0], rows[:, levels]], axis=1))
            west, east = pl.pallas_call(
                edge_kernel,
                grid=(row_count // ROWS,),
                out_shape=(f32(2, CM, LANES), f32(2, CM, LANES)),
                in_specs=[pl.BlockSpec((ROWS, CM, LANES), lambda i: (i, 0, 0))],
                out_specs=(
                    pl.BlockSpec((2, CM, LANES), lambda i: (0, 0, 0)),
                    pl.BlockSpec((2, CM, LANES), lambda i: (0, 0, 0)),
                ),
                scratch_shapes=[pltpu.VMEM((4, CM, LANES), jnp.float32)],
                compiler_params=PARAMS,
                cost_estimate=cost(5),
                name="edges",
            )(rows)
        outgoing = jnp.dot(send_mat, surface, precision=best).reshape(2 * tile_count, slots, 2 * col_count)
        arrived = lax.all_to_all(outgoing, everyone, split_axis=0, concat_axis=0, tiled=True)
        arrived, west, east, diff = lax.optimization_barrier((arrived, west, east, diff))
        force = jnp.dot(take_mat, arrived.reshape(2 * tile_count * slots, 2 * col_count), precision=best)
        pads = jnp.stack(
            [sea_mask, fold_rows, force[:, :col_count], force[:, col_count:], blank, blank, blank, blank], axis=1
        )
        west, east, bottom, top = pl.pallas_call(
            pad_kernel,
            out_shape=(f32(2, CP, LANES), f32(2, CP, LANES), f32(H, CP, LANES), f32(H, CP, LANES)),
            in_specs=[VM, VM, VM, ANY],
            out_specs=(VM, VM, VM, VM),
            scratch_shapes=[pltpu.VMEM((4, CP - CM, LANES), jnp.float32)]
            + [pltpu.VMEM((2, CP - CM, LANES), jnp.float32)] * 2
            + [pltpu.SemaphoreType.DMA((2,))],
            compiler_params=PARAMS,
            cost_estimate=cost(2),
            name="pad_edges",
        )(pads, west, east, rows)
        tops = lax.all_gather(top, "tx", axis=0, tiled=False)
        from_east = shift(west, "tx", -1, True)
        from_west = shift(east, "tx", 1, True)
        low = lax.broadcasted_iota(jnp.int32, (CP, LANES), 1) % 8 < 4
        strip = jnp.where(low, from_west[0], from_east[0])[None]
        from_south = shift(jnp.concatenate([top, strip], axis=0), "ty", 1, False)
        from_north = shift(jnp.concatenate([bottom, strip], axis=0), "ty", -1, False)
        last = interval == INTERVALS - 1
        tile_buffer = pltpu.VMEM((row_count, CP, LANES), jnp.float32)
        inner, sides, near = pl.pallas_call(
            functools.partial(inner_kernel, last),
            out_shape=(
                f32(channels * row_count, col_count) if last else f32(row_count, CM, LANES),
                f32(NSTEP, 2, 2, 2, CP, LANES),
                f32(2, H, CH, LANES),
            ),
            in_specs=[ANY, VM, VM, VM, VM, VM],
            out_specs=(VM, VM, VM),
            scratch_shapes=[tile_buffer] * 4 + [pltpu.VMEM((4, CP, LANES), jnp.float32), pltpu.SemaphoreType.DMA((1,))],
            compiler_params=PARAMS,
            cost_estimate=cost(30),
            name="inner",
        )(rows, pads, from_west, from_east, mix, diff)
        wide = pltpu.VMEM((tx_count, H + 1, CP, LANES), jnp.float32)
        folds = pl.pallas_call(
            fold_kernel,
            out_shape=f32(NSTEP, 2, CP, LANES),
            in_specs=[SM, ANY, VM, VM],
            out_specs=VM,
            scratch_shapes=[
                wide,
                wide,
                pltpu.VMEM((tx_count * LANES, tx_count * LANES), jnp.bfloat16),
                pltpu.VMEM((2 * CP, tx_count * LANES), jnp.bfloat16),
                pltpu.SemaphoreType.DMA((2,)),
            ],
            compiler_params=PARAMS,
            cost_estimate=cost(10),
            name="fold",
        )(info, tops, mix, diff)
        side_buffer = pltpu.VMEM((2, 2 * H + 2, CP, LANES), jnp.float32)
        if last:
            inner = inner.reshape(channels, row_count, col_count)
            done = pltpu.VMEM((2, channels * 8, LANES), jnp.float32)
        else:
            done = pltpu.VMEM((2, H, CM, LANES), jnp.float32)
        rows = pl.pallas_call(
            functools.partial(outer_kernel, last),
            out_shape=f32(*inner.shape),
            in_specs=[SM, VM, VM, VM, VM, VM, VM, VM, ANY],
            out_specs=ANY,
            scratch_shapes=[side_buffer] * 4 + [done, pltpu.SemaphoreType.DMA((2,))],
            input_output_aliases={8: 0},
            compiler_params=PARAMS,
            cost_estimate=cost(5),
            name="outer",
        )(info, sides, near, from_north, from_south, folds, mix, diff, inner)
    return rows.reshape(1, channels, row_count, col_count)


def solution(mesh):
    in_specs = (
        P("comp", None, "ty", "tx"),
        P("comp", None),
        P("comp", None, None),
        P("ty", "tx"),
        P("tx", "ty", None),
        P("tx", "ty"),
        P("tx", "ty"),
        P("tx"),
    )
    out_specs = P("comp", None, "ty", "tx")
    return jax.shard_map(per_device, mesh=mesh, in_specs=in_specs, out_specs=out_specs, check_vma=False)
```
